256 devices in a mesh: section: 8 (over y_lo, x), dp: 8 (over z), tensor: 4 (over y_hi, core).
Axes of the slice: x: 4, y: 4 (y_hi: 2, y_lo: 2; y = y_hi * 2 + y_lo), z: 8, core: 2. Of those that a mesh axis runs over, the one named last changes fastest.
Arguments:
- vision_rows: bfloat16 [8192, 12800], P(('section', 'dp')), may hold values from -100 to 100
- vision_gain: float32 [12800], replicated, may hold values from 0.1 to 1.9
- vision_bias: float32 [12800], replicated, may hold values from -4 to 4
- proj_weight: bfloat16 [12800, 4096], P(('section', 'dp'), 'tensor'), may hold values from -0.0546875 to 0.0546875
- text_rows: bfloat16 [8192, 4096], P(('section', 'dp'), 'tensor'), may hold values from -100 to 100
- text_gain: float32 [4096], P('tensor'), may hold values from 0.1 to 1.9
- slot_of_row: int32 [8192], P(('section', 'dp')), may hold values from -1 to 8191, as said below
- out_cotangent: bfloat16 [8192, 4096], P(('section', 'dp'), 'tensor'), may hold values from -6 to 6
Outputs:
- normed: bfloat16 [8192, 4096], P(('section', 'dp'), 'tensor')
- vision_grad: bfloat16 [8192, 12800], P(('section', 'dp', 'tensor'))
The draws below stay inside these ranges and needn't reach their ends.
Inputs may be any that keep to these rules, and one draw needn't show every extreme that they name: `slot_of_row`: language device g (index g of section+dp) owns slots g * 128 to (g + 1) * 128 - 1. Rows come in aligned runs of 16: a run is all -1 or goes to 16 consecutive slots that start at a multiple of 16. A vision device sends only to language devices with the same dp index, at most 8 // 8 runs to each. No slot receives two rows. In every draw some vision device has all its runs live and some language device receives a row in every slot.
All inputs are finite; a program needn't handle non-finite values.
Results may differ from the reference program's by a relative error of at most 0.0064.
Values may be sent and summed in bfloat16 or wider, within the bound.
No kernel may reach another device: no remote copies, remote signals or barrier semaphores. Data moves between devices by JAX's collectives and lax.ppermute only.
A program may use at most 128 MiB of HBM per device.

```python
import jax
import jax.numpy as jnp
from jax import lax

C = 12800
D = 4096
UNIT = 16
UNITS_DEV = 8
VROWS = 8192
LROWS = 8192
N_SECTION = 8
N_DP = 8


def rough_field(key, row_count, col_count, noise):
    first_key, second_key = jax.random.split(key, 2)
    row_scale = 10.0 ** (jax.random.uniform(first_key, (row_count, 1)) - 0.5)
    ramp = jnp.arange(col_count, dtype=jnp.float32) / max(col_count - 1, 1)
    col_scale = (3.0 ** ramp)[None, :] * 10.0 ** (jax.random.uniform(second_key, (1, col_count)) - 0.5)
    return jnp.clip(noise * row_scale * col_scale, -100.0, 100.0)


def draw_vision_rows(key, part):
    key = jax.random.fold_in(key, 3)
    noise_key, scale_key = jax.random.split(key, 2)
    noise = jax.random.normal(noise_key, (VROWS, C))
    return rough_field(scale_key, VROWS, C, noise).astype(jnp.bfloat16)


def draw_text_rows(key, part):
    key = jax.random.fold_in(key, 5)
    noise_key, scale_key = jax.random.split(key, 2)
    noise = jax.random.normal(noise_key, (LROWS, D))
    return rough_field(scale_key, LROWS, D, noise).astype(jnp.bfloat16)


def one_permutation(key, length):
    return jax.random.permutation(key, length)


def draw_slot_of_row(key, part):
    key = jax.random.fold_in(key, 7)
    keys = jax.random.split(key, 5)
    section_count = N_SECTION
    group_count = N_DP
    unit_count = UNITS_DEV
    orders = jax.vmap(one_permutation, in_axes=(0, None))(jax.random.split(keys[0], group_count), section_count)
    section_ids = jnp.arange(section_count)[:, None, None]
    group_ids = jnp.arange(group_count)[None, :, None]
    unit_ids = jnp.arange(unit_count)[None, None, :]
    offsets = jnp.transpose(orders)[:, :, None]
    target_section = (offsets + unit_ids) % section_count
    layouts = jax.vmap(one_permutation, in_axes=(0, None))(jax.random.split(keys[1], section_count * group_count), unit_count)
    lang_index = target_section * group_count + group_ids
    position = layouts[lang_index, jnp.broadcast_to(unit_ids, lang_index.shape)]
    coins = jax.random.randint(keys[2], (section_count, group_count, unit_count), 0, 100) < 55
    full_sender = jax.random.randint(keys[3], (1, group_count, 1), 0, section_count)
    full_receiver = jax.random.randint(keys[4], (1, group_count, 1), 0, section_count)
    live_units = coins | (section_ids == full_sender) | (target_section == full_receiver)
    run_start = lang_index * (unit_count * UNIT) + position * UNIT
    row_slots = run_start[..., None] + jnp.arange(UNIT)
    return jnp.where(live_units[..., None], row_slots, -1).reshape(-1).astype(jnp.int32)


def level_of(own_key, extent, cuts, least, high):
    level = 1.0
    for axis_at, parts in cuts:
        draws = jax.random.uniform(jax.random.fold_in(jax.random.fold_in(own_key, 6), axis_at), (parts,), jnp.float32, least / len(cuts), high / len(cuts))
        level = level * jnp.repeat(jnp.exp(draws), extent[axis_at] // parts).reshape((-1,) + (1,) * (len(extent) - 1 - axis_at))
    return level


def bell_draw(stream_key, extent, deviation, most, cuts=(), kind=jnp.bfloat16):
    entries = jax.random.normal(stream_key, extent, jnp.float32) * deviation
    if len(cuts) > 0:
        entries = level_of(stream_key, extent, cuts, -0.22, 0.18) * entries
    return jnp.clip(entries, min=-most, max=most).astype(kind)


def setup_inputs(seed: int = 0) -> dict:
    key_list = jax.random.split(jax.random.key(seed), 9)
    return {
        "vision_rows": draw_vision_rows(jax.random.fold_in(key_list[8], 71), 0),
        "vision_gain": jnp.clip(1.0 + 0.18 * jax.random.normal(key_list[1], (C,), jnp.float32), 0.1, 1.9),
        "vision_bias": bell_draw(key_list[2], (C,), 1.0, 4.0, (), jnp.float32),
        "proj_weight": bell_draw(key_list[3], (C, D), C ** -0.5, 0.0546875, ((0, 64), (1, 4))),
        "text_rows": draw_text_rows(jax.random.fold_in(key_list[8], 71), 0),
        "text_gain": jnp.clip(1.0 + 0.18 * jax.random.normal(key_list[5], (D,), jnp.float32), 0.1, 1.9),
        "slot_of_row": draw_slot_of_row(jax.random.fold_in(key_list[8], 71), 0),
        "out_cotangent": bell_draw(key_list[7], (LROWS, D), 1.0, 6.0, ((0, 64), (1, 4))),
    }


VISION_EPS = 1e-05
EPSILON = 1e-06
HALF_ROOT = 0.7071067811865476
INV_ROOT_TWO_PI = 0.3989422804014327

def gelu_value(values):
    return 0.5 * values * (1.0 + lax.erf(values * HALF_ROOT))

def gelu_slope(values):
    return 0.5 * (1.0 + lax.erf(values * HALF_ROOT)) + values * jnp.exp(-0.5 * values * values) * INV_ROOT_TWO_PI

def reference(vision_rows, vision_gain, vision_bias, proj_weight, text_rows, text_gain, slot_of_row, out_cotangent):
    vision_wide = vision_rows.astype(jnp.float32)
    centered = vision_wide - lax.optimization_barrier(jnp.mean(vision_wide, axis=1, keepdims=True))
    vision_inv = lax.rsqrt(lax.optimization_barrier(jnp.mean(centered * centered, axis=1, keepdims=True)) + VISION_EPS)
    vision_hat = centered * vision_inv
    normed_vision = (vision_hat * vision_gain + vision_bias).astype(jnp.bfloat16)
    projected = jnp.dot(normed_vision, proj_weight, preferred_element_type=jnp.float32)
    features = gelu_value(projected).astype(jnp.bfloat16)
    live_rows = slot_of_row >= 0
    target = jnp.where(live_rows, slot_of_row, LROWS).astype(jnp.int32)
    hidden = text_rows.at[target].set(features, mode='drop')
    hidden_wide = hidden.astype(jnp.float32)
    hidden_inv = lax.rsqrt(lax.optimization_barrier(jnp.mean(hidden_wide * hidden_wide, axis=1, keepdims=True)) + EPSILON)
    normed = (hidden_wide * hidden_inv * text_gain).astype(jnp.bfloat16)
    upstream = out_cotangent.astype(jnp.float32) * text_gain
    cross_mean = lax.optimization_barrier(jnp.mean(upstream * hidden_wide, axis=1, keepdims=True))
    hidden_grad = (hidden_inv * (upstream - hidden_wide * hidden_inv * hidden_inv * cross_mean)).astype(jnp.bfloat16)
    source = jnp.where(live_rows, slot_of_row, 0).astype(jnp.int32)
    feature_grad = jnp.where(live_rows[:, None], hidden_grad[source], jnp.zeros((), jnp.bfloat16))
    projected_grad = (feature_grad.astype(jnp.float32) * gelu_slope(projected)).astype(jnp.bfloat16)
    normed_grad = jnp.dot(projected_grad, proj_weight.T, preferred_element_type=jnp.float32)
    weighted = normed_grad * vision_gain
    weighted_mean = lax.optimization_barrier(jnp.mean(weighted, axis=1, keepdims=True))
    vision_cross = lax.optimization_barrier(jnp.mean(weighted * vision_hat, axis=1, keepdims=True))
    vision_grad = vision_inv * (weighted - weighted_mean - vision_hat * vision_cross)
    return (normed, vision_grad.astype(jnp.bfloat16))
```

```python
import functools

import jax
import jax.numpy as jnp
from jax import lax
from jax.experimental import pallas as pl
from jax.experimental.pallas import tpu as pltpu
from jax.sharding import PartitionSpec as P

UNIT = 16
VISION_EPS = 1e-05
EPSILON = 1e-06
HALF_ROOT = 0.7071067811865476
INV_ROOT_TWO_PI = 0.3989422804014327
BF = jnp.bfloat16
F32 = jnp.float32


def norm_kernel(parts, order_ref, rows_ref, gain_ref, bias_ref, out_ref):
    wide = rows_ref[...].astype(F32)
    centered = wide - jnp.mean(wide, axis=1, keepdims=True)
    inv = lax.rsqrt(jnp.mean(centered * centered, axis=1, keepdims=True) + VISION_EPS)
    normed = (centered * inv * gain_ref[...] + bias_ref[...]).astype(BF)
    chunk = normed.shape[1] // parts
    for k in range(parts):
        out_ref[k] = normed[:, k * chunk : (k + 1) * chunk]


def slots_kernel(
    source_ref, live_ref, parts_ref, text_ref, cot_ref, gain_ref, hidden_ref, slope_ref, stat_ref
):
    live = live_ref[pl.program_id(0)] > 0
    projected = parts_ref[0, 0].astype(F32)
    for k in range(1, parts_ref.shape[0]):
        projected = projected + parts_ref[k, 0].astype(F32)
    gate = 0.5 * (1.0 + lax.erf(projected * HALF_ROOT))
    feature = (projected * gate).astype(BF)
    hidden = jnp.where(live, feature, text_ref[...])
    hidden_ref[...] = hidden
    slope_ref[...] = (
        gate + projected * jnp.exp(-0.5 * projected * projected) * INV_ROOT_TWO_PI
    )
    wide = hidden.astype(F32)
    upstream = cot_ref[...].astype(F32) * gain_ref[...]
    square = jnp.sum(wide * wide, axis=1, keepdims=True)
    cross = jnp.sum(upstream * wide, axis=1, keepdims=True)
    lane = lax.broadcasted_iota(jnp.int32, stat_ref.shape, 1)
    stat_ref[...] = jnp.where(lane == 0, square, cross)


def grad_kernel(
    width, source_ref, live_ref, hidden_ref, slope_ref, cot_ref, gain_ref, stat_ref, normed_ref, grad_ref
):
    live = live_ref[pl.program_id(0)] > 0
    stat = stat_ref[...] / width
    inv = lax.rsqrt(stat[:, 0:1] + EPSILON)
    wide = hidden_ref[...].astype(F32)
    normed_ref[...] = (wide * inv * gain_ref[...]).astype(BF)
    upstream = cot_ref[...].astype(F32) * gain_ref[...]
    hidden_grad = (inv * (upstream - wide * inv * inv * stat[:, 1:2])).astype(BF)
    grad = (hidden_grad.astype(F32) * slope_ref[...]).astype(BF)
    grad_ref[0] = jnp.where(live, grad, jnp.zeros_like(grad))


def final_kernel(parts, share_ref, parts_ref, rows_ref, gain_ref, out_ref):
    wide = rows_ref[...].astype(F32)
    centered = wide - jnp.mean(wide, axis=1, keepdims=True)
    inv = lax.rsqrt(jnp.mean(centered * centered, axis=1, keepdims=True) + VISION_EPS)
    hat = centered * inv
    grad = jnp.concatenate([parts_ref[k] for k in range(parts)], axis=1).astype(F32)
    weighted = grad * gain_ref[...]
    weighted_mean = jnp.mean(weighted, axis=1, keepdims=True)
    cross = jnp.mean(weighted * hat, axis=1, keepdims=True)
    out_ref[...] = (inv * (weighted - weighted_mean - hat * cross)).astype(BF)


def shards(
    width, vision_rows, vision_gain, vision_bias, proj_weight, text_rows, text_gain, slot_of_row, out_cotangent
):
    sections = lax.axis_size("section")
    groups = lax.axis_size("dp")
    tensors = lax.axis_size("tensor")
    rows, depth = vision_rows.shape
    slots, columns = text_rows.shape
    units = rows // UNIT
    chunk = depth // sections
    section = lax.axis_index("section")
    tensor = lax.axis_index("tensor")
    lang = section * groups + lax.axis_index("dp")

    gain_row = vision_gain.reshape(1, depth)
    text_gain_row = text_gain.reshape(1, columns)

    unit_slot = slot_of_row.reshape(units, UNIT)[:, 0]
    table = lax.all_to_all(
        jnp.broadcast_to(unit_slot, (sections, units)), "section", 0, 0, tiled=True
    )
    alive = table >= 0
    target = jnp.where(alive, table // (slots * groups), -1)
    places = jnp.arange(units)
    taken = jnp.any(target[:, :, None] == places, axis=1)
    free_rank = jnp.cumsum(~taken, axis=1) - 1
    dead_rank = jnp.cumsum(~alive, axis=1) - 1
    fits = (~taken)[:, None, :] & (free_rank[:, None, :] == dead_rank[:, :, None])
    filler = jnp.sum(jnp.where(fits, places, 0), axis=2)
    place = jnp.where(alive, target, filler).astype(jnp.int32)

    own_alive = unit_slot >= 0
    own_target = jnp.where(own_alive, unit_slot // (slots * groups), -1)
    own_taken = jnp.any(own_target[:, None] == places, axis=0)
    own_fits = (~own_taken)[None, :] & (
        (jnp.cumsum(~own_taken) - 1)[None, :] == (jnp.cumsum(~own_alive) - 1)[:, None]
    )
    own_place = jnp.where(own_alive, own_target, jnp.sum(jnp.where(own_fits, places, 0), axis=1))
    own_order = jnp.sum(
        jnp.where(own_place[:, None] == places, jnp.arange(units)[:, None], 0), axis=0
    ).astype(jnp.int32)

    normed_vision = pl.pallas_call(
        functools.partial(norm_kernel, sections),
        out_shape=jax.ShapeDtypeStruct((sections, rows, chunk), BF),
        grid_spec=pltpu.PrefetchScalarGridSpec(
            num_scalar_prefetch=1,
            grid=(units,),
            in_specs=[
                pl.BlockSpec((UNIT, depth), lambda i, order: (order[i], 0)),
                pl.BlockSpec((1, depth), lambda i, order: (0, 0)),
                pl.BlockSpec((1, depth), lambda i, order: (0, 0)),
            ],
            out_specs=pl.BlockSpec((sections, UNIT, chunk), lambda i, order: (0, i, 0)),
        ),
        compiler_params=pltpu.CompilerParams(vmem_limit_bytes=32 * 2**20),
        name="vision_norm",
    )(own_order, vision_rows, gain_row, vision_bias.reshape(1, depth))
    weight = lax.all_gather(proj_weight, "dp", axis=0, tiled=True)
    arrived = lax.all_to_all(normed_vision, "section", 0, 0, tiled=True)
    partial = jnp.dot(
        arrived.reshape(sections * rows, chunk), weight, preferred_element_type=F32
    ).astype(BF)
    partial = jnp.swapaxes(partial.reshape(sections, units, UNIT, columns), 0, 1)
    partial = lax.all_to_all(
        partial.reshape(units, sections * UNIT, columns), "section", 0, 0, tiled=True
    ).reshape(sections, sections, UNIT, columns)

    mine = alive & (table // slots == lang)
    mine_slot = jnp.sum(jnp.where(mine, table, 0), axis=1)
    has = jnp.any(mine, axis=1)
    local = jnp.where(has, (mine_slot - lang * slots) // UNIT, -1)
    filled = jnp.any(local[:, None] == places, axis=0)
    spare = (~filled)[None, :] & (
        (jnp.cumsum(~filled) - 1)[None, :] == (jnp.cumsum(~has) - 1)[:, None]
    )
    where = jnp.where(has, local, jnp.sum(jnp.where(spare, places, 0), axis=1))
    source = jnp.sum(
        jnp.where(where[:, None] == places, jnp.arange(sections)[:, None], 0), axis=0
    ).astype(jnp.int32)
    filled = filled.astype(jnp.int32)

    row_block = pl.BlockSpec((UNIT, columns), lambda i, source, live: (i, 0))
    gain_block = pl.BlockSpec((1, columns), lambda i, source, live: (0, 0))
    stat_block = pl.BlockSpec((UNIT, 2), lambda i, source, live: (i, 0))
    hidden, slope, stat = pl.pallas_call(
        slots_kernel,
        out_shape=(
            jax.ShapeDtypeStruct((slots, columns), BF),
            jax.ShapeDtypeStruct((slots, columns), F32),
            jax.ShapeDtypeStruct((slots, 2), F32),
        ),
        grid_spec=pltpu.PrefetchScalarGridSpec(
            num_scalar_prefetch=2,
            grid=(slots // UNIT,),
            in_specs=[
                pl.BlockSpec(
                    (sections, 1, UNIT, columns), lambda i, source, live: (0, source[i], 0, 0)
                ),
                row_block,
                row_block,
                gain_block,
            ],
            out_specs=[row_block, row_block, stat_block],
        ),
        name="slots",
    )(source, filled, partial, text_rows, out_cotangent, text_gain_row)
    stat = lax.psum(stat, "tensor")
    normed, grad = pl.pallas_call(
        functools.partial(grad_kernel, width),
        out_shape=(
            jax.ShapeDtypeStruct((slots, columns), BF),
            jax.ShapeDtypeStruct((sections, UNIT, columns), BF),
        ),
        grid_spec=pltpu.PrefetchScalarGridSpec(
            num_scalar_prefetch=2,
            grid=(slots // UNIT,),
            in_specs=[row_block, row_block, row_block, gain_block, stat_block],
            out_specs=[
                row_block,
                pl.BlockSpec((1, UNIT, columns), lambda i, source, live: (source[i], 0, 0)),
            ],
        ),
        name="grads",
    )(source, filled, hidden, slope, out_cotangent, text_gain_row, stat)

    grads = lax.all_to_all(
        jnp.broadcast_to(grad, (sections, sections, UNIT, columns)), "section", 0, 0, tiled=True
    ).reshape(sections * sections, UNIT * columns)
    share = units // tensors
    relative = jnp.array([3, 1, 2, 0]) ^ tensor
    pick = place.reshape(sections, tensors, share)[:, relative]
    pick = pick * sections + jnp.arange(sections)[:, None, None]
    pick = jnp.swapaxes(pick, 0, 1)
    half = sections * rows // 2

    def product(index):
        picked = grads[index.reshape(-1)].reshape(half, columns)
        return lax.dot_general(
            picked, weight, (((1,), (1,)), ((), ())), preferred_element_type=F32
        )

    other_core = [(i, i ^ 1) for i in range(tensors)]
    other_y = [(i, i ^ 2) for i in range(tensors)]
    given = product(pick[:2]).astype(BF)
    got = lax.ppermute(given, "tensor", other_core)
    total = product(pick[2:]) + got.astype(F32)
    quarter = half // 2
    far = lax.ppermute(total[:quarter].astype(BF), "tensor", other_y)
    total = (total[quarter:] + far.astype(F32)).astype(BF)
    back = lax.all_to_all(
        total.reshape(sections, share * UNIT, chunk), "section", 0, 0, tiled=True
    )
    own_rows = rows // tensors
    vision_grad = pl.pallas_call(
        functools.partial(final_kernel, sections),
        out_shape=jax.ShapeDtypeStruct((own_rows, depth), BF),
        grid_spec=pltpu.PrefetchScalarGridSpec(
            num_scalar_prefetch=1,
            grid=(share,),
            in_specs=[
                pl.BlockSpec((sections, UNIT, chunk), lambda i, first: (0, i, 0)),
                pl.BlockSpec((UNIT, depth), lambda i, first: (first[0] + i, 0)),
                pl.BlockSpec((1, depth), lambda i, first: (0, 0)),
            ],
            out_specs=pl.BlockSpec((UNIT, depth), lambda i, first: (i, 0)),
        ),
        compiler_params=pltpu.CompilerParams(vmem_limit_bytes=32 * 2**20),
        name="vision_back",
    )((tensor * share).reshape(1).astype(jnp.int32), back, vision_rows, gain_row)
    return normed, vision_grad


def solution(mesh):
    in_specs = (
        P(("section", "dp"), None),
        P(),
        P(),
        P(("section", "dp"), "tensor"),
        P(("section", "dp"), "tensor"),
        P("tensor"),
        P(("section", "dp")),
        P(("section", "dp"), "tensor"),
    )
    out_specs = (P(("section", "dp"), "tensor"), P(("section", "dp", "tensor"), None))

    def program(*args):
        body = functools.partial(shards, args[4].shape[1])
        return jax.shard_map(
            body, mesh=mesh, in_specs=in_specs, out_specs=out_specs, check_vma=False
        )(*args)

    return program
```

```python
import functools

import jax
import jax.numpy as jnp
from jax import lax
from jax.experimental import pallas as pl
from jax.experimental.pallas import tpu as pltpu
from jax.sharding import PartitionSpec as P

UNIT = 16
LANES = 128
VISION_EPS = 1e-05
EPSILON = 1e-06
HALF_ROOT = 0.7071067811865476
INV_ROOT_TWO_PI = 0.3989422804014327
BF = jnp.bfloat16
F32 = jnp.float32
VMEM = pl.BlockSpec(memory_space=pltpu.VMEM)
SMEM = pl.BlockSpec(memory_space=pltpu.SMEM)
PARAMS = pltpu.CompilerParams(vmem_limit_bytes=40 * 2**20)
NT = (((1,), (1,)), ((), ()))


def shape(dims, dtype):
    return jax.ShapeDtypeStruct(dims, dtype)


def norm_kernel(chunk, order_ref, live_ref, spot_ref, rows_ref, gain_ref, bias_ref, out_ref):
    step = pl.program_id(0)
    wide = rows_ref[...].astype(F32)
    centered = wide - jnp.mean(wide, axis=1, keepdims=True)
    inv = lax.rsqrt(jnp.mean(centered * centered, axis=1, keepdims=True) + VISION_EPS)
    normed = (centered * inv * gain_ref[...] + bias_ref[...]).astype(BF)
    parts, _, padded = out_ref.shape
    lane = lax.broadcasted_iota(jnp.int32, (UNIT, padded - chunk), 1)
    note = jnp.where(lane == 0, order_ref[step], jnp.where(lane == 1, live_ref[step], spot_ref[step]))
    note = note.astype(F32).astype(BF)
    for k in range(parts):
        out_ref[k] = jnp.concatenate([normed[:, k * chunk : (k + 1) * chunk], note], axis=1)


def forward_kernel(core_ref, own_ref, other_ref, weight_ref, out_ref):
    step = pl.program_id(0)
    steps = pl.num_programs(0)

    def work(ref):
        sections, pair, depth = ref.shape
        product = jnp.dot(
            ref[...].reshape(sections * pair, depth), weight_ref[...], preferred_element_type=F32
        ).astype(BF)
        product = product.reshape(sections, pair, product.shape[1])
        for j in range(pair // UNIT):
            out_ref[j] = product[:, j * UNIT : (j + 1) * UNIT].reshape(sections * UNIT, -1)

    @pl.when(step < steps // 2)
    def _():
        work(own_ref)

    @pl.when(step >= steps // 2)
    def _():
        work(other_ref)


def slots_kernel(
    source_ref, live_ref, parts_ref, text_ref, cot_ref, gain_ref, hidden_ref, slope_ref, stat_ref
):
    stats = []
    for q in range(text_ref.shape[0] // UNIT):
        rows = pl.ds(q * UNIT, UNIT)
        from_rows = pl.ds(pl.multiple_of(source_ref[q] * UNIT, UNIT), UNIT)
        projected = parts_ref[0, from_rows].astype(F32)
        for k in range(1, parts_ref.shape[0]):
            projected = projected + parts_ref[k, from_rows].astype(F32)
        gate = 0.5 * (1.0 + lax.erf(projected * HALF_ROOT))
        hidden = jnp.where(live_ref[q] > 0, (projected * gate).astype(BF), text_ref[rows])
        hidden_ref[rows] = hidden
        slope_ref[rows] = gate + projected * jnp.exp(-0.5 * projected * projected) * INV_ROOT_TWO_PI
        wide = hidden.astype(F32)
        upstream = cot_ref[rows].astype(F32) * gain_ref[...]
        square = jnp.sum(wide * wide, axis=1, keepdims=True)
        cross = jnp.sum(upstream * wide, axis=1, keepdims=True)
        lane = lax.broadcasted_iota(jnp.int32, (UNIT, LANES), 1)
        stats.append(jnp.where(lane == 0, square, cross))
    stat_ref[...] = jnp.transpose(jnp.concatenate(stats, axis=0))[: stat_ref.shape[0]]


def row_scales(stat_ref, width):
    stat = stat_ref[...] / width
    pad = jnp.zeros((LANES - stat.shape[0], LANES), F32)
    stat = jnp.transpose(jnp.concatenate([stat, pad], axis=0))
    return lax.rsqrt(stat[:, 0:1] + EPSILON), stat[:, 1:2]


def grad_kernel(
    width, source_ref, live_ref, hidden_ref, slope_ref, cot_ref, gain_ref, stat_ref, grad_ref
):
    inv_all, cross_all = row_scales(stat_ref, width)
    for q in range(hidden_ref.shape[0] // UNIT):
        rows = slice(q * UNIT, (q + 1) * UNIT)
        inv, cross = inv_all[rows], cross_all[rows]
        wide = hidden_ref[rows].astype(F32)
        upstream = cot_ref[rows].astype(F32) * gain_ref[...]
        hidden_grad = (inv * (upstream - wide * inv * inv * cross)).astype(BF)
        grad = (hidden_grad.astype(F32) * slope_ref[rows]).astype(BF)
        grad = jnp.where(live_ref[q] > 0, grad, jnp.zeros_like(grad))
        to_rows = pl.ds(pl.multiple_of(source_ref[q] * UNIT, UNIT), UNIT)
        for k in range(grad_ref.shape[0]):
            grad_ref[k, to_rows] = grad


def normed_kernel(width, hidden_ref, gain_ref, stat_ref, normed_ref):
    inv, _ = row_scales(stat_ref, width)
    normed_ref[...] = (hidden_ref[...].astype(F32) * inv * gain_ref[...]).astype(BF)


def picked(pick_ref, grads_ref, first, count):
    return jnp.concatenate([grads_ref[pick_ref[first + m]] for m in range(count)], axis=0)


def give_kernel(pick_ref, grads_ref, weight_ref, out_ref):
    rows = out_ref.shape[0]
    count = rows // UNIT
    grad = picked(pick_ref, grads_ref, pl.program_id(0) * count, count)
    out_ref[...] = lax.dot_general(grad, weight_ref[...], NT, preferred_element_type=F32).astype(BF)


def far_kernel(first, pick_ref, grads_ref, weight_ref, got_ref, *out_refs):
    grad = picked(pick_ref, grads_ref, first, got_ref.shape[0] // UNIT)
    total = lax.dot_general(grad, weight_ref[...], NT, preferred_element_type=F32)
    total = (total + got_ref[...].astype(F32)).astype(BF)
    rows = out_refs[0].shape[0]
    for j, ref in enumerate(out_refs):
        ref[...] = total[j * rows : (j + 1) * rows]


def near_kernel(first, pick_ref, grads_ref, weight_ref, got_ref, out_ref):
    grad = picked(pick_ref, grads_ref, first, got_ref.shape[0] // UNIT)
    total = lax.dot_general(grad, weight_ref[...], NT, preferred_element_type=F32)
    out_ref[...] = total + got_ref[...].astype(F32)


def sum_kernel(near_ref, *refs):
    out_ref = refs[-1]
    sections, share, _ = out_ref.shape
    rows = refs[0].shape[0]
    for s in range(sections):
        j, at = divmod(s * share, rows)
        far = refs[j][at : at + share].astype(F32)
        out_ref[s] = (near_ref[s * share : (s + 1) * share] + far).astype(BF)


def final_kernel(chunk, first_ref, parts_ref, rows_ref, gain_ref, out_ref):
    wide = rows_ref[...].astype(F32)
    centered = wide - jnp.mean(wide, axis=1, keepdims=True)
    inv = lax.rsqrt(jnp.mean(centered * centered, axis=1, keepdims=True) + VISION_EPS)
    hat = centered * inv
    grad = jnp.concatenate([parts_ref[k][:, :chunk] for k in range(parts_ref.shape[0])], axis=1)
    weighted = grad.astype(F32) * gain_ref[...]
    weighted_mean = jnp.mean(weighted, axis=1, keepdims=True)
    cross = jnp.mean(weighted * hat, axis=1, keepdims=True)
    out_ref[...] = (inv * (weighted - weighted_mean - hat * cross)).astype(BF)


def ring_gather(block, rows):
    groups = lax.axis_size("dp")
    me = lax.axis_index("dp")
    height = block.shape[0]
    up = [(i, (i + 1) % groups) for i in range(groups)]
    down = [(i, (i - 1) % groups) for i in range(groups)]
    out = jnp.zeros((rows, block.shape[1]), block.dtype)

    def put(out, piece, owner, start=0):
        return lax.dynamic_update_slice_in_dim(out, piece, (owner % groups) * height + start, 0)

    out = put(out, block, me)
    rising = falling = block
    full = (groups - 1) // 2
    for hop in range(1, full + 1):
        rising = lax.ppermute(rising, "dp", up)
        falling = lax.ppermute(falling, "dp", down)
        out = put(out, rising, me - hop + groups)
        out = put(out, falling, me + hop)
    if groups % 2 == 0:
        if groups > 1:
            cut = height // 16 * 8
            opposite = me + groups // 2
            out = put(out, lax.ppermute(rising[:cut], "dp", up), opposite)
            out = put(out, lax.ppermute(falling[cut:], "dp", down), opposite, cut)
    return out


def fill_places(wanted, alive, places):
    taken = jnp.any((wanted[..., :, None] == places) & alive[..., :, None], axis=-2)
    free_rank = jnp.cumsum(~taken, axis=-1) - 1
    dead_rank = jnp.cumsum(~alive, axis=-1) - 1
    fits = (~taken)[..., None, :] & (free_rank[..., None, :] == dead_rank[..., :, None])
    filler = jnp.sum(jnp.where(fits, places, 0), axis=-1)
    return jnp.where(alive, wanted, filler).astype(jnp.int32)


def inverse(place, places):
    return jnp.sum(
        jnp.where(place[..., :, None] == places, places[:, None], 0), axis=-2
    ).astype(jnp.int32)


def shards(
    width, vision_rows, vision_gain, vision_bias, proj_weight, text_rows, text_gain, slot_of_row, out_cotangent
):
    sections = lax.axis_size("section")
    groups = lax.axis_size("dp")
    tensors = lax.axis_size("tensor")
    rows, depth = vision_rows.shape
    slots, columns = text_rows.shape
    units = rows // UNIT
    chunk = depth // sections
    padded = -(-(chunk + 3) // LANES) * LANES
    section = lax.axis_index("section")
    tensor = lax.axis_index("tensor")
    core = tensor % 2
    places = jnp.arange(units)
    other_core = [(i, i ^ 1) for i in range(tensors)]
    other_y = [(i, i ^ 2) for i in range(tensors)]

    gain_row = vision_gain.reshape(1, depth)
    text_gain_row = text_gain.reshape(1, columns)
    weight = ring_gather(proj_weight, padded)

    unit_slot = slot_of_row.reshape(units, UNIT)[:, 0]
    alive = unit_slot >= 0
    safe = jnp.where(alive, unit_slot, 0)
    order = inverse(fill_places(safe // (slots * groups), alive, places), places)
    half = units // 2
    own = lax.dynamic_slice_in_dim(order, core * half, half)
    chosen = own[:, None] == places
    live = jnp.sum(jnp.where(chosen, alive, 0), axis=1).astype(jnp.int32)
    spot = jnp.sum(jnp.where(chosen, safe // UNIT % (slots // UNIT), 0), axis=1).astype(jnp.int32)
    sent = pl.pallas_call(
        functools.partial(norm_kernel, chunk),
        out_shape=shape((sections, half * UNIT, padded), BF),
        grid_spec=pltpu.PrefetchScalarGridSpec(
            num_scalar_prefetch=3,
            grid=(half,),
            in_specs=[
                pl.BlockSpec((UNIT, depth), lambda i, order, live, spot: (order[i], 0)),
                pl.BlockSpec((1, depth), lambda i, order, live, spot: (0, 0)),
                pl.BlockSpec((1, depth), lambda i, order, live, spot: (0, 0)),
            ],
            out_specs=pl.BlockSpec(
                (sections, UNIT, padded), lambda i, order, live, spot: (0, i, 0)
            ),
        ),
        compiler_params=PARAMS,
        name="vision_norm",
    )(own, live, spot, vision_rows, gain_row, vision_bias.reshape(1, depth))
    from_own = lax.all_to_all(sent, "section", 0, 0, tiled=True)
    from_other = lax.ppermute(from_own, "tensor", other_core)

    pair = 2 * UNIT
    partial = pl.pallas_call(
        forward_kernel,
        out_shape=shape((units, sections * UNIT, columns), BF),
        grid_spec=pltpu.PrefetchScalarGridSpec(
            num_scalar_prefetch=1,
            grid=(half,),
            in_specs=[
                pl.BlockSpec(
                    (sections, pair, padded), lambda i, core: (0, jnp.minimum(i, half // 2 - 1), 0)
                ),
                pl.BlockSpec(
                    (sections, pair, padded), lambda i, core: (0, jnp.maximum(i - half // 2, 0), 0)
                ),
                pl.BlockSpec((padded, columns), lambda i, core: (0, 0)),
            ],
            out_specs=pl.BlockSpec(
                (2, sections * UNIT, columns),
                lambda i, core: ((i + core[0] * (half // 2)) % half, 0, 0),
            ),
        ),
        compiler_params=PARAMS,
        name="forward",
    )(core.reshape(1).astype(jnp.int32), from_own, from_other, weight)
    partial = lax.all_to_all(partial, "section", 0, 0, tiled=True)

    def notes(array):
        return array[:, ::UNIT, chunk : chunk + 3].astype(jnp.int32)

    first, second = notes(from_own), notes(from_other)
    table = jnp.where(
        core == 0,
        jnp.concatenate([first, second], axis=1),
        jnp.concatenate([second, first], axis=1),
    )
    here = lax.dynamic_slice_in_dim(table, section, 1, 1)[:, 0]
    has = here[:, 1] > 0
    spots = jnp.arange(sections)
    source = inverse(fill_places(here[:, 2], has, spots), spots)
    filled = jnp.sum(jnp.where(source[:, None] == spots, has, 0), axis=1).astype(jnp.int32)
    place = inverse(table[:, :, 0], places)

    hidden, slope, stat = pl.pallas_call(
        slots_kernel,
        out_shape=(
            shape((slots, columns), BF),
            shape((slots, columns), F32),
            shape((8, slots), F32),
        ),
        in_specs=[SMEM, SMEM, VMEM, VMEM, VMEM, VMEM],
        out_specs=(VMEM, VMEM, VMEM),
        compiler_params=PARAMS,
        name="slots",
    )(source, filled, partial, text_rows, out_cotangent, text_gain_row)
    stat = stat + lax.ppermute(stat, "tensor", other_core)
    stat = stat + lax.ppermute(stat, "tensor", other_y)
    grads = pl.pallas_call(
        functools.partial(grad_kernel, width),
        out_shape=shape((sections, sections * UNIT, columns), BF),
        in_specs=[SMEM, SMEM, VMEM, VMEM, VMEM, VMEM, VMEM],
        out_specs=VMEM,
        compiler_params=PARAMS,
        name="grads",
    )(source, filled, hidden, slope, out_cotangent, text_gain_row, stat)
    grads = lax.all_to_all(grads, "section", 0, 0, tiled=True)
    grads = grads.reshape(sections * sections, UNIT, columns)
    normed = pl.pallas_call(
        functools.partial(normed_kernel, width),
        out_shape=shape((slots, columns), BF),
        in_specs=[VMEM, VMEM, VMEM],
        out_specs=VMEM,
        compiler_params=PARAMS,
        name="normed",
    )(hidden, text_gain_row, stat)

    share = units // tensors
    relative = jnp.array([3, 1, 2, 0]) ^ tensor
    runs = relative[:, None] * share + jnp.arange(share)
    hit = runs[:, None, :, None] == places
    pick = jnp.sum(jnp.where(hit, place[None, :, None, :], 0), axis=3)
    pick = (pick * sections + spots[None, :, None]).reshape(-1).astype(jnp.int32)
    quarter = sections * share * UNIT
    runs_quarter = sections * share
    whole = [SMEM, VMEM, VMEM]
    given = pl.pallas_call(
        give_kernel,
        out_shape=shape((2 * quarter, padded), BF),
        grid_spec=pltpu.PrefetchScalarGridSpec(
            num_scalar_prefetch=1,
            grid=(2,),
            in_specs=[
                pl.BlockSpec((sections * sections, UNIT, columns), lambda i, pick: (0, 0, 0)),
                pl.BlockSpec((padded, columns), lambda i, pick: (0, 0)),
            ],
            out_specs=pl.BlockSpec((quarter, padded), lambda i, pick: (i, 0)),
        ),
        compiler_params=PARAMS,
        name="give",
    )(pick, grads, weight)
    got = lax.ppermute(given, "tensor", other_core)
    pieces = 4
    far = pl.pallas_call(
        functools.partial(far_kernel, 2 * runs_quarter),
        out_shape=tuple(shape((quarter // pieces, padded), BF) for _ in range(pieces)),
        grid=(1,),
        in_specs=[
            SMEM,
            pl.BlockSpec((sections * sections, UNIT, columns), lambda i: (0, 0, 0)),
            pl.BlockSpec((padded, columns), lambda i: (0, 0)),
            pl.BlockSpec((quarter, padded), lambda i: (0, 0)),
        ],
        out_specs=tuple(
            pl.BlockSpec((quarter // pieces, padded), lambda i: (0, 0)) for _ in range(pieces)
        ),
        compiler_params=PARAMS,
        name="far",
    )(pick, grads, weight, got)
    far = [lax.ppermute(piece, "tensor", other_y) for piece in far]
    near = pl.pallas_call(
        functools.partial(near_kernel, 3 * runs_quarter),
        out_shape=shape((quarter, padded), F32),
        grid=(1,),
        in_specs=[
            SMEM,
            pl.BlockSpec((sections * sections, UNIT, columns), lambda i: (0, 0, 0)),
            pl.BlockSpec((padded, columns), lambda i: (0, 0)),
            pl.BlockSpec((quarter, padded), lambda i: (1, 0)),
        ],
        out_specs=pl.BlockSpec((quarter, padded), lambda i: (0, 0)),
        compiler_params=PARAMS,
        name="near",
    )(pick, grads, weight, got)
    total = pl.pallas_call(
        sum_kernel,
        out_shape=shape((sections, share * UNIT, padded), BF),
        in_specs=[VMEM] * (1 + pieces),
        out_specs=VMEM,
        compiler_params=PARAMS,
        name="total",
    )(near, *far)
    back = lax.all_to_all(total, "section", 0, 0, tiled=True)
    vision_grad = pl.pallas_call(
        functools.partial(final_kernel, chunk),
        out_shape=shape((share * UNIT, depth), BF),
        grid_spec=pltpu.PrefetchScalarGridSpec(
            num_scalar_prefetch=1,
            grid=(share,),
            in_specs=[
                pl.BlockSpec((sections, UNIT, padded), lambda i, first: (0, i, 0)),
                pl.BlockSpec((UNIT, depth), lambda i, first: (first[0] + i, 0)),
                pl.BlockSpec((1, depth), lambda i, first: (0, 0)),
            ],
            out_specs=pl.BlockSpec((UNIT, depth), lambda i, first: (i, 0)),
        ),
        compiler_params=PARAMS,
        name="vision_back",
    )((tensor * share).reshape(1).astype(jnp.int32), back, vision_rows, gain_row)
    return normed, vision_grad


def solution(mesh):
    in_specs = (
        P(("section", "dp"), None),
        P(),
        P(),
        P(("section", "dp"), "tensor"),
        P(("section", "dp"), "tensor"),
        P("tensor"),
        P(("section", "dp")),
        P(("section", "dp"), "tensor"),
    )
    out_specs = (P(("section", "dp"), "tensor"), P(("section", "dp", "tensor"), None))

    def program(*args):
        body = functools.partial(shards, args[4].shape[1])
        return jax.shard_map(
            body, mesh=mesh, in_specs=in_specs, out_specs=out_specs, check_vma=False
        )(*args)

    return program
```

```python
import functools

import jax
import jax.numpy as jnp
from jax import lax
from jax.experimental import pallas as pl
from jax.experimental.pallas import tpu as pltpu
from jax.sharding import Mesh
from jax.sharding import PartitionSpec as P

UNIT = 16
LANES = 128
VISION_EPS = 1e-05
EPSILON = 1e-06
HALF_ROOT = 0.7071067811865476
INV_ROOT_TWO_PI = 0.3989422804014327
BF = jnp.bfloat16
F32 = jnp.float32
VMEM = pl.BlockSpec(memory_space=pltpu.VMEM)
SMEM = pl.BlockSpec(memory_space=pltpu.SMEM)
ANY = pl.BlockSpec(memory_space=pl.ANY)
FREE = pl.CostEstimate(flops=0, transcendentals=0, bytes_accessed=0)
PARAMS = pltpu.CompilerParams(vmem_limit_bytes=40 * 2**20)
WIDE = pltpu.CompilerParams(vmem_limit_bytes=60 * 2**20)
NT = (((1,), (1,)), ((), ()))


def shape(dims, dtype):
    return jax.ShapeDtypeStruct(dims, dtype)


def norm_kernel(chunk, order_ref, live_ref, spot_ref, rows_ref, gain_ref, bias_ref, out_ref):
    step = pl.program_id(0)
    wide = rows_ref[...].astype(F32)
    centered = wide - jnp.mean(wide, axis=1, keepdims=True)
    inv = lax.rsqrt(jnp.mean(centered * centered, axis=1, keepdims=True) + VISION_EPS)
    gain, bias = gain_ref[...].reshape(1, -1), bias_ref[...].reshape(1, -1)
    normed = (centered * inv * gain + bias).astype(BF)
    parts, _, padded = out_ref.shape
    lane = lax.broadcasted_iota(jnp.int32, (UNIT, padded - chunk), 1)
    note = jnp.where(lane == 0, order_ref[step], jnp.where(lane == 1, live_ref[step], spot_ref[step]))
    note = note.astype(F32).astype(BF)
    for k in range(parts):
        out_ref[k] = jnp.concatenate([normed[:, k * chunk : (k + 1) * chunk], note], axis=1)


def forward_kernel(core_ref, own_ref, other_ref, weight_ref, out_ref, note_ref):
    step = pl.program_id(0)
    steps = pl.num_programs(0)

    def work(ref):
        sections, high, depth = ref.shape
        product = jnp.dot(
            ref[...].reshape(sections * high, depth), weight_ref[...], preferred_element_type=F32
        ).astype(BF)
        product = product.reshape(sections, high, product.shape[1])
        for j in range(high // UNIT):
            out_ref[j] = product[:, j * UNIT : (j + 1) * UNIT].reshape(sections * UNIT, -1)
            heads = [ref[s, j * UNIT : (j + 1) * UNIT, depth - LANES :][:1] for s in range(sections)]
            note_ref[j] = jnp.concatenate([head.astype(F32) for head in heads], axis=0)

    @pl.when(step < steps // 2)
    def _():
        work(own_ref)

    @pl.when(step >= steps // 2)
    def _():
        work(other_ref)


def prepare_kernel(text_ref, cot_ref, gain_ref, upstream_ref, stat_ref):
    upstream_ref[...] = cot_ref[...].astype(F32) * gain_ref[...]
    text = text_ref[...].astype(F32)
    square = jnp.sum(text * text, axis=1, keepdims=True)
    square = jnp.broadcast_to(square, (square.shape[0], LANES))
    stat_ref[...] = jnp.transpose(square)[: stat_ref.shape[0]]


def slots_kernel(place_ref, pick_ref, parts_ref, upstream_ref, text_stat_ref, feature_ref, slope_ref, stat_ref):
    del pick_ref
    lane = lax.broadcasted_iota(jnp.int32, (UNIT, LANES), 1)
    stats = []
    for s in range(feature_ref.shape[0] // UNIT):
        rows = slice(s * UNIT, (s + 1) * UNIT)
        projected = parts_ref[0, rows].astype(F32)
        for k in range(1, parts_ref.shape[0]):
            projected = projected + parts_ref[k, rows].astype(F32)
        gate = 0.5 * (1.0 + lax.erf(projected * HALF_ROOT))
        feature = (projected * gate).astype(BF)
        feature_ref[rows] = feature
        slope_ref[rows] = gate + projected * jnp.exp(-0.5 * projected * projected) * INV_ROOT_TWO_PI
        wide = feature.astype(F32)
        at = pl.ds(pl.multiple_of(place_ref[s] * UNIT, UNIT), UNIT)
        square = jnp.sum(wide * wide, axis=1, keepdims=True)
        cross = jnp.sum(upstream_ref[at] * wide, axis=1, keepdims=True)
        stats.append(jnp.where(lane == 0, square, cross))
    stat = jnp.transpose(jnp.concatenate(stats, axis=0))[: stat_ref.shape[0]]
    row = lax.broadcasted_iota(jnp.int32, stat.shape, 0)
    stat_ref[...] = jnp.where(row == 2, text_stat_ref[...], stat)


def row_scales(stat_refs, width):
    stat = sum(ref[...] for ref in stat_refs) / width
    pad = jnp.zeros((LANES - stat.shape[0], LANES), F32)
    return jnp.transpose(jnp.concatenate([stat, pad], axis=0))


def grad_kernel(
    width, place_ref, live_ref, feature_ref, slope_ref, upstream_ref, *refs
):
    stat_refs, grad_ref = refs[:-1], refs[-1]
    stat = row_scales(stat_refs, width)
    for s in range(feature_ref.shape[0] // UNIT):
        rows = slice(s * UNIT, (s + 1) * UNIT)
        inv, cross = lax.rsqrt(stat[rows, 0:1] + EPSILON), stat[rows, 1:2]
        wide = feature_ref[rows].astype(F32)
        at = pl.ds(pl.multiple_of(place_ref[s] * UNIT, UNIT), UNIT)
        hidden_grad = (inv * (upstream_ref[at] - wide * inv * inv * cross)).astype(BF)
        grad = (hidden_grad.astype(F32) * slope_ref[rows]).astype(BF)
        grad = jnp.where(live_ref[s] > 0, grad, jnp.zeros_like(grad))
        for k in range(grad_ref.shape[0]):
            grad_ref[k, rows] = grad


def normed_kernel(
    width, place_ref, live_ref, text_ref, feature_ref, gain_ref, *refs
):
    stat_refs, normed_ref = refs[:-1], refs[-1]
    stat = row_scales(stat_refs, width)
    inv = lax.rsqrt(stat[:, 2:3] + EPSILON)
    normed_ref[...] = (text_ref[...].astype(F32) * inv * gain_ref[...]).astype(BF)
    for s in range(feature_ref.shape[0] // UNIT):
        rows = slice(s * UNIT, (s + 1) * UNIT)
        at = pl.ds(pl.multiple_of(place_ref[s] * UNIT, UNIT), UNIT)

        @pl.when(live_ref[s] > 0)
        def _(rows=rows, at=at):
            inv = lax.rsqrt(stat[rows, 0:1] + EPSILON)
            normed_ref[at] = (feature_ref[rows].astype(F32) * inv * gain_ref[...]).astype(BF)


def give_kernel(first, pick_ref, grads_ref, weight_ref, out_ref):
    count = out_ref.shape[0] // UNIT
    grad = jnp.concatenate([grads_ref[pick_ref[first + m]] for m in range(count)], axis=0)
    out_ref[...] = lax.dot_general(grad, weight_ref[...], NT, preferred_element_type=F32).astype(BF)


def keep_kernel(first, pick_ref, grads_ref, weight_ref, low_ref, high_ref, out_ref):
    targets, share, _ = out_ref.shape
    count = targets * share // UNIT
    start = first + pl.program_id(0) * count
    grad = jnp.concatenate([grads_ref[pick_ref[start + m]] for m in range(count)], axis=0)
    total = lax.dot_general(grad, weight_ref[...], NT, preferred_element_type=F32)
    got = jnp.where(pl.program_id(0) == 0, low_ref[...], high_ref[...])
    total = (total + got.astype(F32)).astype(BF)
    for j in range(targets):
        out_ref[j] = total[j * share : (j + 1) * share]


def final_kernel(chunk, first_ref, parts_ref, rows_ref, gain_ref, out_ref):
    wide = rows_ref[...].astype(F32)
    centered = wide - jnp.mean(wide, axis=1, keepdims=True)
    inv = lax.rsqrt(jnp.mean(centered * centered, axis=1, keepdims=True) + VISION_EPS)
    hat = centered * inv
    grad = jnp.concatenate(
        [
            parts_ref[k][:, :chunk].astype(F32) + parts_ref[k + 1][:, :chunk].astype(F32)
            for k in range(0, parts_ref.shape[0], 2)
        ],
        axis=1,
    )
    weighted = grad * gain_ref[...].reshape(1, -1)
    weighted_mean = jnp.mean(weighted, axis=1, keepdims=True)
    cross = jnp.mean(weighted * hat, axis=1, keepdims=True)
    out_ref[...] = (inv * (weighted - weighted_mean - hat * cross)).astype(BF)


def ring_gather(block, rows, beside):
    groups = lax.axis_size("dp")
    me = lax.axis_index("dp")
    height = block.shape[0]
    up = [(i, (i + 1) % groups) for i in range(groups)]
    down = [(i, (i - 1) % groups) for i in range(groups)]
    out = jnp.zeros((rows, block.shape[1]), block.dtype)

    def put(out, piece, owner):
        return lax.dynamic_update_slice_in_dim(out, piece, owner % groups * height, 0)

    out = put(out, block, me)
    rising = falling = block
    for hop in range(1, (groups - 1) // 2 + 1):
        rising = lax.ppermute(rising, "dp", up)
        falling = lax.ppermute(falling, "dp", down)
        out, rising, falling = lax.optimization_barrier((out, rising, falling))
        if hop == 1:
            rising, falling, beside = lax.optimization_barrier((rising, falling, beside))
        out = put(out, rising, me - hop + groups)
        out = put(out, falling, me + hop)
    if groups % 2 == 0:
        out = put(out, lax.ppermute(rising, "dp", up), me + groups // 2)
    return out, rising, falling, beside


def fill_places(wanted, alive, places):
    taken = jnp.any((wanted[..., :, None] == places) & alive[..., :, None], axis=-2)
    free_rank = jnp.cumsum(~taken, axis=-1) - 1
    dead_rank = jnp.cumsum(~alive, axis=-1) - 1
    fits = (~taken)[..., None, :] & (free_rank[..., None, :] == dead_rank[..., :, None])
    filler = jnp.sum(jnp.where(fits, places, 0), axis=-1)
    return jnp.where(alive, wanted, filler).astype(jnp.int32)


def inverse(place, places):
    return jnp.sum(
        jnp.where(place[..., :, None] == places, places[:, None], 0), axis=-2
    ).astype(jnp.int32)


def shards(
    width, vision_rows, vision_gain, vision_bias, proj_weight, text_rows, text_gain, slot_of_row, out_cotangent
):
    sections = lax.axis_size("section")
    groups = lax.axis_size("dp")
    tensors = 2 * lax.axis_size("y_hi")
    rows, depth = vision_rows.shape
    slots, columns = text_rows.shape
    units = rows // UNIT
    chunk = depth // sections
    padded = -(-(chunk + 3) // LANES) * LANES
    section = lax.axis_index("section")
    core = lax.axis_index("core")
    tensor = lax.axis_index("y_hi") * 2 + core
    places = jnp.arange(units)
    swap_core = [(0, 1), (1, 0)]

    text_gain_row = text_gain.reshape(1, columns)

    unit_slot = slot_of_row.reshape(units, UNIT)[:, 0]
    alive = unit_slot >= 0
    safe = jnp.where(alive, unit_slot, 0)
    order = inverse(fill_places(safe // (slots * groups), alive, places), places)
    half = units // 2
    own = lax.dynamic_slice_in_dim(order, core * half, half)
    chosen = own[:, None] == places
    live = jnp.sum(jnp.where(chosen, alive, 0), axis=1).astype(jnp.int32)
    spot = jnp.sum(jnp.where(chosen, safe // UNIT % (slots // UNIT), 0), axis=1).astype(jnp.int32)
    sent = pl.pallas_call(
        functools.partial(norm_kernel, chunk),
        out_shape=pltpu.HBM((sections, half * UNIT, padded), BF),
        grid_spec=pltpu.PrefetchScalarGridSpec(
            num_scalar_prefetch=3,
            grid=(half,),
            in_specs=[
                pl.BlockSpec((UNIT, depth), lambda i, order, live, spot: (order[i], 0)),
                pl.BlockSpec((depth,), lambda i, order, live, spot: (0,)),
                pl.BlockSpec((depth,), lambda i, order, live, spot: (0,)),
            ],
            out_specs=pl.BlockSpec(
                (sections, UNIT, padded), lambda i, order, live, spot: (0, i, 0)
            ),
        ),
        compiler_params=WIDE,
        cost_estimate=FREE,
        name="vision_norm",
    )(own, live, spot, vision_rows, vision_gain, vision_bias)
    weight, rising, falling, sent = ring_gather(proj_weight, padded, sent)
    from_own = lax.all_to_all(sent, "section", 0, 0, tiled=True)
    from_own, *_ = lax.optimization_barrier((from_own, rising, falling))
    from_other = lax.ppermute(from_own, "core", swap_core)

    pair = 2 * UNIT
    spread = lambda i, core: ((i + core[0] * (half // 2)) % half, 0, 0)
    partial, table = pl.pallas_call(
        forward_kernel,
        out_shape=(
            pltpu.HBM((units, sections * UNIT, columns), BF),
            shape((units, sections, LANES), F32),
        ),
        grid_spec=pltpu.PrefetchScalarGridSpec(
            num_scalar_prefetch=1,
            grid=(half,),
            in_specs=[
                pl.BlockSpec(
                    (sections, pair, padded), lambda i, core: (0, jnp.minimum(i, half // 2 - 1), 0)
                ),
                pl.BlockSpec(
                    (sections, pair, padded), lambda i, core: (0, jnp.maximum(i - half // 2, 0), 0)
                ),
                pl.BlockSpec((padded, columns), lambda i, core: (0, 0)),
            ],
            out_specs=(
                pl.BlockSpec((2, sections * UNIT, columns), spread),
                pl.BlockSpec((2, sections, LANES), spread),
            ),
        ),
        compiler_params=PARAMS,
        cost_estimate=FREE,
        name="forward",
    )(core.reshape(1).astype(jnp.int32), from_own, from_other, weight)
    partial = lax.all_to_all(partial, "section", 0, 0, tiled=True)

    at = LANES - (padded - chunk)
    table = jnp.swapaxes(table[:, :, at : at + 3], 0, 1).astype(jnp.int32)
    here = lax.dynamic_slice_in_dim(table, section, 1, 1)[:, 0]
    has = here[:, 1] > 0
    spots = jnp.arange(sections)
    where = fill_places(here[:, 2], has, spots)
    has = has.astype(jnp.int32)
    place = inverse(table[:, :, 0], places)

    share = units // tensors
    runs = (jnp.arange(2)[::-1] ^ core)[:, None, None]
    runs = (2 * jnp.arange(2)[None, :, None] + runs) * share + jnp.arange(share)
    hit = runs[:, None, :, :, None] == places
    pick = jnp.sum(jnp.where(hit, place[None, :, None, None, :], 0), axis=4)
    pick = (pick * sections + spots[None, :, None, None]).reshape(-1).astype(jnp.int32)
    upstream, text_stat = pl.pallas_call(
        prepare_kernel,
        out_shape=(shape((slots, columns), F32), shape((8, LANES), F32)),
        in_specs=[VMEM] * 3,
        out_specs=(VMEM, VMEM),
        compiler_params=PARAMS,
        cost_estimate=FREE,
        name="prepare",
    )(text_rows, out_cotangent, text_gain_row)
    feature, slope, stat = pl.pallas_call(
        slots_kernel,
        out_shape=(
            shape((slots, columns), BF),
            shape((slots, columns), F32),
            shape((8, LANES), F32),
        ),
        in_specs=[SMEM, ANY, VMEM, VMEM, VMEM],
        out_specs=(VMEM, VMEM, VMEM),
        compiler_params=PARAMS,
        cost_estimate=FREE,
        name="slots",
    )(where, pick, partial, upstream, text_stat)
    stats = [stat] + [
        lax.ppermute(stat, ("y_hi", "core"), [(i, i ^ turn) for i in range(tensors)])
        for turn in range(1, tensors)
    ]
    grads = pl.pallas_call(
        functools.partial(grad_kernel, width),
        out_shape=pltpu.HBM((sections, slots, columns), BF),
        in_specs=[SMEM, SMEM] + [VMEM] * (3 + tensors),
        out_specs=VMEM,
        compiler_params=PARAMS,
        cost_estimate=FREE,
        name="grads",
    )(where, has, feature, slope, upstream, *stats)
    grads = lax.all_to_all(grads, "section", 0, 0, tiled=True)
    grads = grads.reshape(sections * sections, UNIT, columns)
    normed = pl.pallas_call(
        functools.partial(normed_kernel, width),
        out_shape=shape((slots, columns), BF),
        in_specs=[SMEM, SMEM] + [VMEM] * (3 + tensors),
        out_specs=VMEM,
        compiler_params=PARAMS,
        cost_estimate=FREE,
        name="normed",
    )(where, has, text_rows, feature, text_gain_row, *stats)

    targets = sections * 2
    runs_half = sections * units // 4
    full = [
        SMEM,
        pl.BlockSpec((sections * sections, UNIT, columns), lambda *i: (0, 0, 0)),
        pl.BlockSpec((padded, columns), lambda *i: (0, 0)),
    ]
    got = []
    for h in range(2):
        given = pl.pallas_call(
            functools.partial(give_kernel, h * runs_half),
            out_shape=shape((runs_half * UNIT, padded), BF),
            in_specs=[SMEM, VMEM, VMEM],
            out_specs=VMEM,
            compiler_params=PARAMS,
            cost_estimate=FREE,
            name=f"give{h}",
        )(pick, grads, weight)
        got.append(lax.ppermute(given, "core", swap_core))
    total = pl.pallas_call(
        functools.partial(keep_kernel, 2 * runs_half),
        out_shape=pltpu.HBM((targets, share * UNIT, padded), BF),
        grid=(2,),
        in_specs=full + [pl.BlockSpec((runs_half * UNIT, padded), lambda i: (0, 0))] * 2,
        out_specs=pl.BlockSpec((sections, share * UNIT, padded), lambda i: (i, 0, 0)),
        compiler_params=PARAMS,
        cost_estimate=FREE,
        name="keep",
    )(pick, grads, weight, *got)
    back = lax.all_to_all(total, ("section", "y_hi"), 0, 0, tiled=True)
    vision_grad = pl.pallas_call(
        functools.partial(final_kernel, chunk),
        out_shape=shape((share * UNIT, depth), BF),
        grid_spec=pltpu.PrefetchScalarGridSpec(
            num_scalar_prefetch=1,
            grid=(share,),
            in_specs=[
                pl.BlockSpec((targets, UNIT, padded), lambda i, first: (0, i, 0)),
                pl.BlockSpec((UNIT, depth), lambda i, first: (first[0] + i, 0)),
                pl.BlockSpec((depth,), lambda i, first: (0,)),
            ],
            out_specs=pl.BlockSpec((UNIT, depth), lambda i, first: (i, 0)),
        ),
        compiler_params=WIDE,
        cost_estimate=FREE,
        name="vision_back",
    )((tensor * share).reshape(1).astype(jnp.int32), back, vision_rows, vision_gain)
    return normed, vision_grad


def solution(mesh):
    mesh = Mesh(
        mesh.devices.reshape(mesh.shape["section"], mesh.shape["dp"], -1, 2),
        ("section", "dp", "y_hi", "core"),
    )
    tensor = ("y_hi", "core")
    in_specs = (
        P(("section", "dp"), None),
        P(),
        P(),
        P(("section", "dp"), tensor),
        P(("section", "dp"), tensor),
        P(tensor),
        P(("section", "dp")),
        P(("section", "dp"), tensor),
    )
    out_specs = (P(("section", "dp"), tensor), P(("section", "dp", *tensor), None))

    def program(*args):
        body = functools.partial(shards, args[4].shape[1])
        return jax.shard_map(
            body, mesh=mesh, in_specs=in_specs, out_specs=out_specs, check_vma=False
        )(*args)

    return program
```

```python
import functools

import jax
import jax.numpy as jnp
from jax import lax
from jax.experimental import pallas as pl
from jax.experimental.pallas import tpu as pltpu
from jax.sharding import Mesh
from jax.sharding import PartitionSpec as P

UNIT = 16
LANES = 128
VISION_EPS = 1e-05
EPSILON = 1e-06
HALF_ROOT = 0.7071067811865476
INV_ROOT_TWO_PI = 0.3989422804014327
BF = jnp.bfloat16
F32 = jnp.float32
VMEM = pl.BlockSpec(memory_space=pltpu.VMEM)
SMEM = pl.BlockSpec(memory_space=pltpu.SMEM)
ANY = pl.BlockSpec(memory_space=pl.ANY)
FREE = pl.CostEstimate(flops=0, transcendentals=0, bytes_accessed=0)
PARAMS = pltpu.CompilerParams(vmem_limit_bytes=40 * 2**20)
WIDE = pltpu.CompilerParams(vmem_limit_bytes=60 * 2**20)
NT = (((1,), (1,)), ((), ()))


def shape(dims, dtype):
    return jax.ShapeDtypeStruct(dims, dtype)


def norm_kernel(chunk, order_ref, live_ref, spot_ref, rows_ref, gain_ref, bias_ref, out_ref):
    step = pl.program_id(0)
    wide = rows_ref[...].astype(F32)
    centered = wide - jnp.mean(wide, axis=1, keepdims=True)
    inv = lax.rsqrt(jnp.mean(centered * centered, axis=1, keepdims=True) + VISION_EPS)
    gain, bias = gain_ref[...].reshape(1, -1), bias_ref[...].reshape(1, -1)
    normed = (centered * inv * gain + bias).astype(BF)
    parts, _, padded = out_ref.shape
    lane = lax.broadcasted_iota(jnp.int32, (UNIT, padded - chunk), 1)
    note = jnp.where(lane == 0, order_ref[step], jnp.where(lane == 1, live_ref[step], spot_ref[step]))
    note = note.astype(F32).astype(BF)
    for k in range(parts):
        at = (k % 2 * (parts // 2) + k // 2) * chunk
        out_ref[k] = jnp.concatenate([normed[:, at : at + chunk], note], axis=1)


def forward_kernel(core_ref, tile_ref, own_ref, other_ref, weight_ref, out_ref, window_ref, note_ref):
    step = pl.program_id(0)
    steps = pl.num_programs(0)

    def work(ref):
        sections, high, depth = ref.shape
        at = pl.ds(pl.multiple_of(tile_ref[0] * LANES, LANES), window_ref.shape[2])
        product = jnp.dot(
            ref[...].reshape(sections * high, depth), weight_ref[...], preferred_element_type=F32
        )
        product = product.reshape(sections, high, product.shape[1])
        for j in range(high // UNIT):
            rows = product[:, j * UNIT : (j + 1) * UNIT].reshape(sections * UNIT, -1)
            out_ref[j] = rows
            run = slice(j * UNIT, (j + 1) * UNIT)
            window_ref[j] = ref[:, run, at].reshape(sections * UNIT, -1)
            heads = [ref[s, run, depth - LANES :][:1] for s in range(sections)]
            note_ref[j] = jnp.concatenate([head.astype(F32) for head in heads], axis=0)

    @pl.when(step < steps // 2)
    def _():
        work(own_ref)

    @pl.when(step >= steps // 2)
    def _():
        work(other_ref)


def tail_kernel(window_ref, weight_ref, main_ref, out_ref):
    for target in range(out_ref.shape[0]):
        product = jnp.dot(window_ref[target], weight_ref[...], preferred_element_type=F32)
        out_ref[target] = (main_ref[target] + product).astype(BF)


def prepare_kernel(text_ref, cot_ref, gain_ref, upstream_ref, stat_ref):
    upstream_ref[...] = cot_ref[...].astype(F32) * gain_ref[...]
    text = text_ref[...].astype(F32)
    square = jnp.sum(text * text, axis=1, keepdims=True)
    square = jnp.broadcast_to(square, (square.shape[0], LANES))
    stat_ref[...] = jnp.transpose(square)[: stat_ref.shape[0]]


def slots_kernel(
    place_ref, pick_ref, hat_ref, parts_ref, upstream_ref, text_stat_ref, feature_ref, slope_ref, stat_ref
):
    del pick_ref, hat_ref
    lane = lax.broadcasted_iota(jnp.int32, (UNIT, LANES), 1)
    stats = []
    for s in range(feature_ref.shape[0] // UNIT):
        rows = slice(s * UNIT, (s + 1) * UNIT)
        projected = parts_ref[0, rows].astype(F32)
        for k in range(1, parts_ref.shape[0]):
            projected = projected + parts_ref[k, rows].astype(F32)
        gate = 0.5 * (1.0 + lax.erf(projected * HALF_ROOT))
        feature = (projected * gate).astype(BF)
        feature_ref[rows] = feature
        slope_ref[rows] = gate + projected * jnp.exp(-0.5 * projected * projected) * INV_ROOT_TWO_PI
        wide = feature.astype(F32)
        at = pl.ds(pl.multiple_of(place_ref[s] * UNIT, UNIT), UNIT)
        square = jnp.sum(wide * wide, axis=1, keepdims=True)
        cross = jnp.sum(upstream_ref[at] * wide, axis=1, keepdims=True)
        stats.append(jnp.where(lane == 0, square, cross))
    stat = jnp.transpose(jnp.concatenate(stats, axis=0))[: stat_ref.shape[0]]
    row = lax.broadcasted_iota(jnp.int32, stat.shape, 0)
    stat_ref[...] = jnp.where(row == 2, text_stat_ref[...], stat)


def row_scales(stat_refs, width):
    stat = sum(ref[...] for ref in stat_refs) / width
    pad = jnp.zeros((LANES - stat.shape[0], LANES), F32)
    return jnp.transpose(jnp.concatenate([stat, pad], axis=0))


def grad_kernel(
    width, place_ref, live_ref, feature_ref, slope_ref, upstream_ref, *refs
):
    stat_refs, grad_ref = refs[:-1], refs[-1]
    stat = row_scales(stat_refs, width)
    for s in range(feature_ref.shape[0] // UNIT):
        rows = slice(s * UNIT, (s + 1) * UNIT)
        inv, cross = lax.rsqrt(stat[rows, 0:1] + EPSILON), stat[rows, 1:2]
        wide = feature_ref[rows].astype(F32)
        at = pl.ds(pl.multiple_of(place_ref[s] * UNIT, UNIT), UNIT)
        hidden_grad = (inv * (upstream_ref[at] - wide * inv * inv * cross)).astype(BF)
        grad = (hidden_grad.astype(F32) * slope_ref[rows]).astype(BF)
        grad = jnp.where(live_ref[s] > 0, grad, jnp.zeros_like(grad))
        grad_ref[s] = grad


def normed_kernel(
    width, place_ref, live_ref, text_ref, feature_ref, gain_ref, *refs
):
    stat_refs, normed_ref = refs[:-1], refs[-1]
    stat = row_scales(stat_refs, width)
    inv = lax.rsqrt(stat[:, 2:3] + EPSILON)
    normed_ref[...] = (text_ref[...].astype(F32) * inv * gain_ref[...]).astype(BF)
    for s in range(feature_ref.shape[0] // UNIT):
        rows = slice(s * UNIT, (s + 1) * UNIT)
        at = pl.ds(pl.multiple_of(place_ref[s] * UNIT, UNIT), UNIT)

        @pl.when(live_ref[s] > 0)
        def _(rows=rows, at=at):
            inv = lax.rsqrt(stat[rows, 0:1] + EPSILON)
            normed_ref[at] = (feature_ref[rows].astype(F32) * inv * gain_ref[...]).astype(BF)


def arrange_kernel(pick_ref, *refs):
    blocks, out_ref = refs[:-1], refs[-1]
    for b, ref in enumerate(blocks):
        for s in range(ref.shape[0]):
            out_ref[pick_ref[b * ref.shape[0] + s]] = ref[s]


def back_kernel(grads_ref, weight_ref, out_ref):
    grad = grads_ref[...].reshape(out_ref.shape[0], -1)
    product = lax.dot_general(grad, weight_ref[...], NT, preferred_element_type=F32)
    out_ref[...] = product.astype(out_ref.dtype)


def join_kernel(own_ref, low_ref, high_ref, out_ref):
    got = jnp.where(pl.program_id(0) == 0, low_ref[...], high_ref[...])
    total = (own_ref[...] + got.astype(F32)).astype(BF)
    targets, share, _ = out_ref.shape
    for j in range(targets):
        out_ref[j] = total[j * share : (j + 1) * share]


def hat_kernel(first_ref, table_ref, rows_ref, hat_ref, inv_ref):
    del table_ref
    wide = rows_ref[...].astype(F32)
    centered = wide - jnp.mean(wide, axis=1, keepdims=True)
    inv = lax.rsqrt(jnp.mean(centered * centered, axis=1, keepdims=True) + VISION_EPS)
    hat_ref[...] = centered * inv
    inv_ref[...] = jnp.broadcast_to(inv, inv_ref.shape)


def final_kernel(chunk, order, parts_ref, hat_ref, inv_ref, gain_ref, out_ref):
    grad = jnp.concatenate(
        [
            parts_ref[a][:, :chunk].astype(F32) + parts_ref[b][:, :chunk].astype(F32)
            for a, b in order
        ],
        axis=1,
    )
    hat, inv = hat_ref[...], inv_ref[:, 0:1]
    weighted = grad * gain_ref[...].reshape(1, -1)
    weighted_mean = jnp.mean(weighted, axis=1, keepdims=True)
    cross = jnp.mean(weighted * hat, axis=1, keepdims=True)
    out_ref[...] = (inv * (weighted - weighted_mean - hat * cross)).astype(BF)


def after_kernel(array_ref, before_ref, out_ref):
    del array_ref, before_ref, out_ref


def ring_gather(block, rows, beside):
    groups = lax.axis_size("dp")
    me = lax.axis_index("dp")
    height = block.shape[0]
    up = [(i, (i + 1) % groups) for i in range(groups)]
    down = [(i, (i - 1) % groups) for i in range(groups)]
    out = jnp.zeros((rows, block.shape[1]), block.dtype)

    def put(out, piece, owner):
        return lax.dynamic_update_slice_in_dim(out, piece, owner % groups * height, 0)

    out = put(out, block, me)
    rising = falling = rising_once = block
    for hop in range(1, (groups - 1) // 2 + 1):
        rising = lax.ppermute(rising, "dp", up)
        falling = lax.ppermute(falling, "dp", down)
        out, rising, falling = lax.optimization_barrier((out, rising, falling))
        if hop == 1:
            rising, falling, beside = lax.optimization_barrier((rising, falling, beside))
            rising_once = rising
        out = put(out, rising, me - hop + groups)
        out = put(out, falling, me + hop)
    last = lax.ppermute(rising, "dp", up)
    owner = (me + groups // 2) % groups
    return out, last, owner * height, rising, falling, rising_once, beside


def fill_places(wanted, alive, places):
    taken = jnp.any((wanted[..., :, None] == places) & alive[..., :, None], axis=-2)
    free_rank = jnp.cumsum(~taken, axis=-1) - 1
    dead_rank = jnp.cumsum(~alive, axis=-1) - 1
    fits = (~taken)[..., None, :] & (free_rank[..., None, :] == dead_rank[..., :, None])
    filler = jnp.sum(jnp.where(fits, places, 0), axis=-1)
    return jnp.where(alive, wanted, filler).astype(jnp.int32)


def inverse(place, places):
    return jnp.sum(
        jnp.where(place[..., :, None] == places, places[:, None], 0), axis=-2
    ).astype(jnp.int32)


def shards(
    width, vision_rows, vision_gain, vision_bias, proj_weight, text_rows, text_gain, slot_of_row, out_cotangent
):
    along = lax.axis_size("x")
    sections = 2 * along
    along_first = ("x", "y_lo")
    groups = lax.axis_size("dp")
    tensors = 2 * lax.axis_size("y_hi")
    rows, depth = vision_rows.shape
    slots, columns = text_rows.shape
    units = rows // UNIT
    chunk = depth // sections
    padded = -(-(chunk + 3) // LANES) * LANES
    y_lo = lax.axis_index("y_lo")
    section = lax.axis_index("x") * 2 + y_lo
    core = lax.axis_index("core")
    tensor = lax.axis_index("y_hi") * 2 + core
    places = jnp.arange(units)
    swap_core = [(0, 1), (1, 0)]

    text_gain_row = text_gain.reshape(1, columns)

    unit_slot = slot_of_row.reshape(units, UNIT)[:, 0]
    alive = unit_slot >= 0
    safe = jnp.where(alive, unit_slot, 0)
    target = safe // (slots * groups)
    target = target % along * 2 + target // along
    order = inverse(fill_places(target, alive, places), places)
    half = units // 2
    own = lax.dynamic_slice_in_dim(order, core * half, half)
    chosen = own[:, None] == places
    live = jnp.sum(jnp.where(chosen, alive, 0), axis=1).astype(jnp.int32)
    spot = jnp.sum(jnp.where(chosen, safe // UNIT % (slots // UNIT), 0), axis=1).astype(jnp.int32)
    sent = pl.pallas_call(
        functools.partial(norm_kernel, chunk),
        out_shape=pltpu.HBM((sections, half * UNIT, padded), BF),
        grid_spec=pltpu.PrefetchScalarGridSpec(
            num_scalar_prefetch=3,
            grid=(half,),
            in_specs=[
                pl.BlockSpec((UNIT, depth), lambda i, order, live, spot: (order[i], 0)),
                pl.BlockSpec((depth,), lambda i, order, live, spot: (0,)),
                pl.BlockSpec((depth,), lambda i, order, live, spot: (0,)),
            ],
            out_specs=pl.BlockSpec(
                (sections, UNIT, padded), lambda i, order, live, spot: (0, i, 0)
            ),
        ),
        compiler_params=WIDE,
        cost_estimate=FREE,
        name="vision_norm",
    )(own, live, spot, vision_rows, vision_gain, vision_bias)
    early_weight, last, last_row, rising, falling, rising_once, sent = ring_gather(proj_weight, padded, sent)
    sent = pl.pallas_call(
        after_kernel,
        out_shape=pltpu.HBM(sent.shape, sent.dtype),
        in_specs=[ANY, ANY],
        out_specs=ANY,
        input_output_aliases={0: 0},
        cost_estimate=FREE,
        name="after",
    )(sent, rising_once)
    from_own = lax.all_to_all(sent, along_first, 0, 0, tiled=True)
    from_own, *_ = lax.optimization_barrier((from_own, rising, falling))
    from_other = lax.ppermute(from_own, "core", swap_core)

    pair = 2 * UNIT
    spread = lambda i, *_: ((i + _[0][0] * (half // 2)) % half, 0, 0)
    sides = [
        pl.BlockSpec((sections, pair, padded), lambda i, *_: (0, jnp.minimum(i, half // 2 - 1), 0)),
        pl.BlockSpec((sections, pair, padded), lambda i, *_: (0, jnp.maximum(i - half // 2, 0), 0)),
    ]
    core_index = core.reshape(1).astype(jnp.int32)
    height = last.shape[0]
    window = -(-(height + LANES - 8) // LANES) * LANES
    tile = jnp.minimum(last_row // LANES, (padded - window) // LANES).astype(jnp.int32)
    main, x_window, table = pl.pallas_call(
        forward_kernel,
        out_shape=(
            shape((units, sections * UNIT, columns), F32),
            shape((units, sections * UNIT, window), BF),
            shape((units, sections, LANES), F32),
        ),
        grid_spec=pltpu.PrefetchScalarGridSpec(
            num_scalar_prefetch=2,
            grid=(half,),
            in_specs=sides + [pl.BlockSpec((padded, columns), lambda i, *_: (0, 0))],
            out_specs=(
                pl.BlockSpec((2, sections * UNIT, columns), spread),
                pl.BlockSpec((2, sections * UNIT, window), spread),
                pl.BlockSpec((2, sections, LANES), spread),
            ),
        ),
        compiler_params=PARAMS,
        cost_estimate=FREE,
        name="forward",
    )(core_index, tile.reshape(1), from_own, from_other, early_weight)
    last_window = lax.dynamic_update_slice_in_dim(
        jnp.zeros((window, columns), BF), last, last_row - tile * LANES, 0
    )
    partial = pl.pallas_call(
        tail_kernel,
        out_shape=pltpu.HBM((units, sections * UNIT, columns), BF),
        in_specs=[VMEM, VMEM, VMEM],
        out_specs=VMEM,
        compiler_params=PARAMS,
        cost_estimate=FREE,
        name="tail",
    )(x_window, last_window, main)
    partial = lax.all_to_all(partial, along_first, 0, 0, tiled=True)
    weight = lax.dynamic_update_slice_in_dim(early_weight, last, last_row, 0)

    at = LANES - (padded - chunk)
    table = jnp.swapaxes(table[:, :, at : at + 3], 0, 1).astype(jnp.int32)
    here = lax.dynamic_slice_in_dim(table, section, 1, 1)[:, 0]
    has = here[:, 1] > 0
    spots = jnp.arange(sections)
    where = fill_places(here[:, 2], has, spots)
    has = has.astype(jnp.int32)

    share = units // tensors
    back = jnp.array([0, 0, 1, 1, -1, -1, 2, 2])
    from_section = (section // 2 - back) % along * 2 + (y_lo ^ jnp.array([0, 1] * 4))
    run = jnp.sum(
        jnp.where(from_section[:, None, None] == spots, table[None, :, :, 0], 0), axis=2
    )
    side = run // share
    pick = (side % 2 == core) * along + spots // 2
    pick = ((pick * 2 + side // 2) * 2 + spots % 2) * share + run % share
    pick = pick.reshape(-1).astype(jnp.int32)
    hat, hat_inv = pl.pallas_call(
        hat_kernel,
        out_shape=(shape((share * UNIT, depth), F32), shape((share * UNIT, LANES), F32)),
        grid_spec=pltpu.PrefetchScalarGridSpec(
            num_scalar_prefetch=1,
            grid=(share,),
            in_specs=[ANY, pl.BlockSpec((UNIT, depth), lambda i, first: (first[0] + i, 0))],
            out_specs=(
                pl.BlockSpec((UNIT, depth), lambda i, first: (i, 0)),
                pl.BlockSpec((UNIT, LANES), lambda i, first: (i, 0)),
            ),
        ),
        compiler_params=WIDE,
        cost_estimate=FREE,
        name="vision_hat",
    )((tensor * share).reshape(1).astype(jnp.int32), table, vision_rows)
    upstream, text_stat = pl.pallas_call(
        prepare_kernel,
        out_shape=(shape((slots, columns), F32), shape((8, LANES), F32)),
        in_specs=[VMEM] * 3,
        out_specs=(VMEM, VMEM),
        compiler_params=PARAMS,
        cost_estimate=FREE,
        name="prepare",
    )(text_rows, out_cotangent, text_gain_row)
    feature, slope, stat = pl.pallas_call(
        slots_kernel,
        out_shape=(
            shape((slots, columns), BF),
            shape((slots, columns), F32),
            shape((8, LANES), F32),
        ),
        in_specs=[SMEM, ANY, ANY, VMEM, VMEM, VMEM],
        out_specs=(VMEM, VMEM, VMEM),
        compiler_params=PARAMS,
        cost_estimate=FREE,
        name="slots",
    )(where, pick, hat, partial, upstream, text_stat)
    stats = [stat] + [
        lax.ppermute(stat, ("y_hi", "core"), [(i, i ^ turn) for i in range(tensors)])
        for turn in range(1, tensors)
    ]
    grads = pl.pallas_call(
        functools.partial(grad_kernel, width),
        out_shape=shape((sections, UNIT, columns), BF),
        in_specs=[SMEM, SMEM] + [VMEM] * (3 + tensors),
        out_specs=VMEM,
        compiler_params=PARAMS,
        cost_estimate=FREE,
        name="grads",
    )(where, has, feature, slope, upstream, *stats)
    def turn(block, dx, dy=0):
        moves = [
            (i, (i // along ^ dy) * along + (i + dx) % along) for i in range(sections)
        ]
        return lax.ppermute(block, ("y_lo", "x"), moves)

    across = turn(grads, 0, 1)
    left, right = lax.optimization_barrier((turn(grads, 1), turn(grads, -1)))
    left_across, right_across = turn(across, 1), turn(across, -1)
    opposite, opposite_across = turn(left, 1), turn(right_across, -1)
    blocks = [grads, across, left, left_across, right, right_across, opposite, opposite_across]
    grads = pl.pallas_call(
        arrange_kernel,
        out_shape=shape((sections * sections, UNIT, columns), BF),
        in_specs=[SMEM] + [VMEM] * sections,
        out_specs=VMEM,
        compiler_params=PARAMS,
        cost_estimate=FREE,
        name="arrange",
    )(pick, *blocks)
    normed = pl.pallas_call(
        functools.partial(normed_kernel, width),
        out_shape=shape((slots, columns), BF),
        in_specs=[SMEM, SMEM] + [VMEM] * (3 + tensors),
        out_specs=VMEM,
        compiler_params=PARAMS,
        cost_estimate=FREE,
        name="normed",
    )(where, has, text_rows, feature, text_gain_row, *stats)

    peers = sections * 2
    quarter = sections * units // 4

    def product(first, count, dtype, name):
        return pl.pallas_call(
            back_kernel,
            out_shape=shape((count * quarter * UNIT, padded), dtype),
            grid=(count,),
            in_specs=[
                pl.BlockSpec((quarter, UNIT, columns), lambda i: (first + i, 0, 0)),
                pl.BlockSpec((padded, columns), lambda i: (0, 0)),
            ],
            out_specs=pl.BlockSpec((quarter * UNIT, padded), lambda i: (i, 0)),
            compiler_params=PARAMS,
            cost_estimate=FREE,
            name=name,
        )(grads, weight)

    got = [
        lax.ppermute(product(h, 1, BF, f"give{h}"), "core", swap_core) for h in range(2)
    ]
    total = pl.pallas_call(
        join_kernel,
        out_shape=pltpu.HBM((peers, share * UNIT, padded), BF),
        grid=(2,),
        in_specs=[pl.BlockSpec((quarter * UNIT, padded), lambda i: (i, 0))]
        + [pl.BlockSpec((quarter * UNIT, padded), lambda i: (0, 0))] * 2,
        out_specs=pl.BlockSpec((sections, share * UNIT, padded), lambda i: (i, 0, 0)),
        compiler_params=PARAMS,
        cost_estimate=FREE,
        name="join",
    )(product(2, 2, F32, "keep"), *got)
    back = lax.all_to_all(total, ("x", "y_hi", "y_lo"), 0, 0, tiled=True)
    order = []
    for y_lo in range(2):
        for x in range(along):
            order.append([(x * 2 + y_hi) * 2 + y_lo for y_hi in range(2)])
    vision_grad = pl.pallas_call(
        functools.partial(final_kernel, chunk, order),
        out_shape=shape((share * UNIT, depth), BF),
        grid=(share,),
        in_specs=[
            pl.BlockSpec((peers, UNIT, padded), lambda i: (0, i, 0)),
            pl.BlockSpec((UNIT, depth), lambda i: (i, 0)),
            pl.BlockSpec((UNIT, LANES), lambda i: (i, 0)),
            pl.BlockSpec((depth,), lambda i: (0,)),
        ],
        out_specs=pl.BlockSpec((UNIT, depth), lambda i: (i, 0)),
        compiler_params=PARAMS,
        cost_estimate=FREE,
        name="vision_back",
    )(back, hat, hat_inv, vision_gain)
    return normed, vision_grad


def solution(mesh):
    mesh = Mesh(
        mesh.devices.reshape(2, mesh.shape["section"] // 2, mesh.shape["dp"], -1, 2),
        ("y_lo", "x", "dp", "y_hi", "core"),
    )
    rows, tensor = ("y_lo", "x", "dp"), ("y_hi", "core")
    in_specs = (
        P(rows, None),
        P(),
        P(),
        P(rows, tensor),
        P(rows, tensor),
        P(tensor),
        P(rows),
        P(rows, tensor),
    )
    out_specs = (P(rows, tensor), P((*rows, *tensor), None))

    def program(*args):
        body = functools.partial(shards, args[4].shape[1])
        return jax.shard_map(
            body, mesh=mesh, in_specs=in_specs, out_specs=out_specs, check_vma=False
        )(*args)

    return program
```

```python
import functools

import jax
import jax.numpy as jnp
from jax import lax
from jax.experimental import pallas as pl
from jax.experimental.pallas import tpu as pltpu
from jax.sharding import Mesh
from jax.sharding import PartitionSpec as P

UNIT = 16
LANES = 128
VISION_EPS = 1e-05
EPSILON = 1e-06
HALF_ROOT = 0.7071067811865476
INV_ROOT_TWO_PI = 0.3989422804014327
BF = jnp.bfloat16
F32 = jnp.float32
VMEM = pl.BlockSpec(memory_space=pltpu.VMEM)
SMEM = pl.BlockSpec(memory_space=pltpu.SMEM)
ANY = pl.BlockSpec(memory_space=pl.ANY)
FREE = pl.CostEstimate(flops=0, transcendentals=0, bytes_accessed=0)
PARAMS = pltpu.CompilerParams(vmem_limit_bytes=40 * 2**20)
WIDE = pltpu.CompilerParams(vmem_limit_bytes=60 * 2**20)
NT = (((1,), (1,)), ((), ()))


def shape(dims, dtype):
    return jax.ShapeDtypeStruct(dims, dtype)


def run_order(slot_ref, units, section_slots, along):
    slots = [slot_ref[u * UNIT] for u in range(units)]
    alive = [slot >= 0 for slot in slots]
    target = [jnp.maximum(slot, 0) // section_slots for slot in slots]
    target = [t % along * 2 + t // along for t in target]
    place = [jnp.where(a, t, -1) for a, t in zip(alive, target)]
    taken = []
    for spot in range(units):
        hits = [jnp.where(p == spot, 1, 0) for p in place]
        taken.append(functools.reduce(lambda a, b: a + b, hits))
    dead_rank = jnp.int32(0)
    for u in range(units):
        free_rank = jnp.int32(0)
        filler = jnp.int32(0)
        for spot in range(units):
            free = 1 - taken[spot]
            filler = jnp.where((free > 0) & (free_rank == dead_rank), spot, filler)
            free_rank = free_rank + free
        place[u] = jnp.where(alive[u], place[u], filler)
        dead_rank = dead_rank + jnp.where(alive[u], 0, 1)
    return slots, alive, place


def norm_kernel(
    chunk, own_slots, section_slots, along, slot_ref, core_ref, rows_ref, gain_ref, bias_ref, out_ref, held, sems
):
    parts, high, padded = out_ref.shape
    half = high // UNIT
    units = 2 * half
    slots, alive, place = run_order(slot_ref, units, section_slots, along)
    notes = []
    for i in range(half):
        run, slot, live = jnp.int32(0), jnp.int32(0), jnp.int32(0)
        for u in range(units):
            here = place[u] == core_ref[0] * half + i
            run = jnp.where(here, u, run)
            slot = jnp.where(here, slots[u], slot)
            live = jnp.where(here & alive[u], 1, live)
        spot = jnp.where(live > 0, slot // UNIT % (own_slots // UNIT), 0)
        notes.append((run, live, spot))
    copies = []
    for i, (run, _, _) in enumerate(notes):
        rows = pl.ds(pl.multiple_of(run * UNIT, UNIT), UNIT)
        copies.append(pltpu.make_async_copy(rows_ref.at[rows], held.at[i], sems.at[i]))
        copies[i].start()
    gain, bias = gain_ref[...].reshape(1, -1), bias_ref[...].reshape(1, -1)
    lane = lax.broadcasted_iota(jnp.int32, (UNIT, padded - chunk), 1)
    for i, (run, live, spot) in enumerate(notes):
        copies[i].wait()
        wide = held[i].astype(F32)
        centered = wide - jnp.mean(wide, axis=1, keepdims=True)
        inv = lax.rsqrt(jnp.mean(centered * centered, axis=1, keepdims=True) + VISION_EPS)
        normed = (centered * inv * gain + bias).astype(BF)
        note = jnp.where(lane == 0, run, jnp.where(lane == 1, live, spot)).astype(F32).astype(BF)
        for k in range(parts):
            at = (k % 2 * (parts // 2) + k // 2) * chunk
            out_ref[k, i * UNIT : (i + 1) * UNIT] = jnp.concatenate(
                [normed[:, at : at + chunk], note], axis=1
            )


def forward_kernel(tile_ref, rows_ref, weight_ref, out_ref, window_ref, note_ref):
    sections, high, depth = rows_ref.shape
    at = pl.ds(pl.multiple_of(tile_ref[0] * LANES, LANES), window_ref.shape[2])
    product = jnp.dot(
        rows_ref[...].reshape(sections * high, depth), weight_ref[...], preferred_element_type=F32
    )
    product = product.reshape(sections, high, product.shape[1])
    for j in range(high // UNIT):
        run = slice(j * UNIT, (j + 1) * UNIT)
        out_ref[j] = product[:, run].reshape(sections * UNIT, -1)
        window_ref[j] = rows_ref[:, run, at].reshape(sections * UNIT, -1)
        heads = [rows_ref[s, run, depth - LANES :][:1] for s in range(sections)]
        note_ref[j] = jnp.concatenate([head.astype(F32) for head in heads], axis=0)


def tail_kernel(core_ref, own_window_ref, other_window_ref, weight_ref, own_ref, other_ref, out_ref):
    half = own_ref.shape[0]
    halves = ((core_ref[0], own_window_ref, own_ref), (1 - core_ref[0], other_window_ref, other_ref))
    for side, window_ref, main_ref in halves:
        for j in range(half):
            product = jnp.dot(window_ref[j], weight_ref[...], preferred_element_type=F32)
            out_ref[side * half + j] = (main_ref[j] + product).astype(BF)


def prepare_kernel(before_ref, text_ref, cot_ref, gain_ref, upstream_ref, stat_ref):
    del before_ref
    upstream_ref[...] = cot_ref[...].astype(F32) * gain_ref[...]
    text = text_ref[...].astype(F32)
    square = jnp.sum(text * text, axis=1, keepdims=True)
    square = jnp.broadcast_to(square, (square.shape[0], LANES))
    stat_ref[...] = jnp.transpose(square)[: stat_ref.shape[0]]


def slots_kernel(
    place_ref, pick_ref, hat_ref, parts_ref, upstream_ref, text_stat_ref, feature_ref, slope_ref, stat_ref
):
    del pick_ref, hat_ref
    lane = lax.broadcasted_iota(jnp.int32, (UNIT, LANES), 1)
    stats = []
    for s in range(feature_ref.shape[0] // UNIT):
        rows = slice(s * UNIT, (s + 1) * UNIT)
        projected = parts_ref[0, rows].astype(F32)
        for k in range(1, parts_ref.shape[0]):
            projected = projected + parts_ref[k, rows].astype(F32)
        gate = 0.5 * (1.0 + lax.erf(projected * HALF_ROOT))
        feature = (projected * gate).astype(BF)
        feature_ref[rows] = feature
        slope_ref[rows] = gate + projected * jnp.exp(-0.5 * projected * projected) * INV_ROOT_TWO_PI
        wide = feature.astype(F32)
        at = pl.ds(pl.multiple_of(place_ref[s] * UNIT, UNIT), UNIT)
        square = jnp.sum(wide * wide, axis=1, keepdims=True)
        cross = jnp.sum(upstream_ref[at] * wide, axis=1, keepdims=True)
        stats.append(jnp.where(lane == 0, square, cross))
    stat = jnp.transpose(jnp.concatenate(stats, axis=0))[: stat_ref.shape[0]]
    row = lax.broadcasted_iota(jnp.int32, stat.shape, 0)
    stat_ref[...] = jnp.where(row == 2, text_stat_ref[...], stat)


def row_scales(stat_refs, width):
    stat = sum(ref[...] for ref in stat_refs) / width
    pad = jnp.zeros((LANES - stat.shape[0], LANES), F32)
    return jnp.transpose(jnp.concatenate([stat, pad], axis=0))


def grad_kernel(
    width, place_ref, live_ref, feature_ref, slope_ref, upstream_ref, *refs
):
    stat_refs, grad_ref = refs[:-1], refs[-1]
    stat = row_scales(stat_refs, width)
    for s in range(feature_ref.shape[0] // UNIT):
        rows = slice(s * UNIT, (s + 1) * UNIT)
        inv, cross = lax.rsqrt(stat[rows, 0:1] + EPSILON), stat[rows, 1:2]
        wide = feature_ref[rows].astype(F32)
        at = pl.ds(pl.multiple_of(place_ref[s] * UNIT, UNIT), UNIT)
        hidden_grad = (inv * (upstream_ref[at] - wide * inv * inv * cross)).astype(BF)
        grad = (hidden_grad.astype(F32) * slope_ref[rows]).astype(BF)
        grad = jnp.where(live_ref[s] > 0, grad, jnp.zeros_like(grad))
        grad_ref[s] = grad


def normed_kernel(
    width, place_ref, live_ref, text_ref, feature_ref, gain_ref, *refs
):
    stat_refs, normed_ref = refs[:-1], refs[-1]
    stat = row_scales(stat_refs, width)
    inv = lax.rsqrt(stat[:, 2:3] + EPSILON)
    normed_ref[...] = (text_ref[...].astype(F32) * inv * gain_ref[...]).astype(BF)
    for s in range(feature_ref.shape[0] // UNIT):
        rows = slice(s * UNIT, (s + 1) * UNIT)
        at = pl.ds(pl.multiple_of(place_ref[s] * UNIT, UNIT), UNIT)

        @pl.when(live_ref[s] > 0)
        def _(rows=rows, at=at):
            inv = lax.rsqrt(stat[rows, 0:1] + EPSILON)
            normed_ref[at] = (feature_ref[rows].astype(F32) * inv * gain_ref[...]).astype(BF)


def arrange_kernel(pick_ref, *refs):
    blocks, out_ref = refs[:-1], refs[-1]
    for b, ref in enumerate(blocks):
        for s in range(ref.shape[0]):
            out_ref[pick_ref[b * ref.shape[0] + s]] = ref[s]


def back_kernel(grads_ref, weight_ref, out_ref):
    grad = grads_ref[...].reshape(out_ref.shape[0], -1)
    product = lax.dot_general(grad, weight_ref[...], NT, preferred_element_type=F32)
    out_ref[...] = product.astype(out_ref.dtype)


def join_kernel(own_ref, low_ref, high_ref, out_ref):
    got = jnp.where(pl.program_id(0) == 0, low_ref[...], high_ref[...])
    total = (own_ref[...] + got.astype(F32)).astype(BF)
    targets, share, _ = out_ref.shape
    for j in range(targets):
        out_ref[j] = total[j * share : (j + 1) * share]


def hat_kernel(first_ref, table_ref, rows_ref, hat_ref, inv_ref):
    del table_ref
    wide = rows_ref[...].astype(F32)
    centered = wide - jnp.mean(wide, axis=1, keepdims=True)
    inv = lax.rsqrt(jnp.mean(centered * centered, axis=1, keepdims=True) + VISION_EPS)
    hat_ref[...] = centered * inv
    inv_ref[...] = jnp.broadcast_to(inv, inv_ref.shape)


def final_kernel(chunk, order, parts_ref, hat_ref, inv_ref, gain_ref, out_ref):
    grad = jnp.concatenate(
        [
            parts_ref[a][:, :chunk].astype(F32) + parts_ref[b][:, :chunk].astype(F32)
            for a, b in order
        ],
        axis=1,
    )
    hat, inv = hat_ref[...], inv_ref[:, 0:1]
    weighted = grad * gain_ref[...].reshape(1, -1)
    weighted_mean = jnp.mean(weighted, axis=1, keepdims=True)
    cross = jnp.mean(weighted * hat, axis=1, keepdims=True)
    out_ref[...] = (inv * (weighted - weighted_mean - hat * cross)).astype(BF)


def ring_gather(block, rows, beside):
    groups = lax.axis_size("dp")
    me = lax.axis_index("dp")
    height = block.shape[0]
    up = [(i, (i + 1) % groups) for i in range(groups)]
    down = [(i, (i - 1) % groups) for i in range(groups)]
    out = jnp.zeros((rows, block.shape[1]), block.dtype)

    def put(out, piece, owner):
        return lax.dynamic_update_slice_in_dim(out, piece, owner % groups * height, 0)

    out = put(out, block, me)
    rising = falling = block
    for hop in range(1, (groups - 1) // 2 + 1):
        rising = lax.ppermute(rising, "dp", up)
        falling = lax.ppermute(falling, "dp", down)
        out, rising, falling = lax.optimization_barrier((out, rising, falling))
        if hop == 1:
            rising, falling, beside = lax.optimization_barrier((rising, falling, beside))
        out = put(out, rising, me - hop + groups)
        out = put(out, falling, me + hop)
    last = lax.ppermute(rising, "dp", up)
    owner = (me + groups // 2) % groups
    return out, last, owner * height, rising, falling, beside


def fill_places(wanted, alive, places):
    taken = jnp.any((wanted[..., :, None] == places) & alive[..., :, None], axis=-2)
    free_rank = jnp.cumsum(~taken, axis=-1) - 1
    dead_rank = jnp.cumsum(~alive, axis=-1) - 1
    fits = (~taken)[..., None, :] & (free_rank[..., None, :] == dead_rank[..., :, None])
    filler = jnp.sum(jnp.where(fits, places, 0), axis=-1)
    return jnp.where(alive, wanted, filler).astype(jnp.int32)


def inverse(place, places):
    return jnp.sum(
        jnp.where(place[..., :, None] == places, places[:, None], 0), axis=-2
    ).astype(jnp.int32)


def shards(
    width, vision_rows, vision_gain, vision_bias, proj_weight, text_rows, text_gain, slot_of_row, out_cotangent
):
    along = lax.axis_size("x")
    sections = 2 * along
    along_first = ("x", "y_lo")
    groups = lax.axis_size("dp")
    tensors = 2 * lax.axis_size("y_hi")
    rows, depth = vision_rows.shape
    slots, columns = text_rows.shape
    units = rows // UNIT
    chunk = depth // sections
    padded = -(-(chunk + 3) // LANES) * LANES
    y_lo = lax.axis_index("y_lo")
    section = lax.axis_index("x") * 2 + y_lo
    core = lax.axis_index("core")
    tensor = lax.axis_index("y_hi") * 2 + core
    places = jnp.arange(units)
    swap_core = [(0, 1), (1, 0)]

    text_gain_row = text_gain.reshape(1, columns)

    half = units // 2
    core_index = core.reshape(1).astype(jnp.int32)
    sent = pl.pallas_call(
        functools.partial(norm_kernel, chunk, slots, slots * groups, along),
        out_shape=pltpu.HBM((sections, half * UNIT, padded), BF),
        in_specs=[SMEM, SMEM, ANY, VMEM, VMEM],
        out_specs=VMEM,
        scratch_shapes=[pltpu.VMEM((half, UNIT, depth), BF), pltpu.SemaphoreType.DMA((half,))],
        compiler_params=WIDE,
        cost_estimate=FREE,
        name="vision_norm",
    )(slot_of_row, core_index, vision_rows, vision_gain, vision_bias)
    early_weight, last, last_row, rising, falling, sent = ring_gather(proj_weight, padded, sent)
    from_own = lax.all_to_all(sent, along_first, 0, 0, tiled=True)
    from_own, *_ = lax.optimization_barrier((from_own, rising, falling))
    from_other = lax.ppermute(from_own, "core", swap_core)

    pair = 2 * UNIT
    height = last.shape[0]
    window = -(-(height + LANES - 8) // LANES) * LANES
    tile = jnp.minimum(last_row // LANES, (padded - window) // LANES).astype(jnp.int32)

    def forward(rows, name):
        return pl.pallas_call(
            forward_kernel,
            out_shape=(
                shape((half, sections * UNIT, columns), F32),
                shape((half, sections * UNIT, window), BF),
                shape((half, sections, LANES), F32),
            ),
            grid_spec=pltpu.PrefetchScalarGridSpec(
                num_scalar_prefetch=1,
                grid=(half // 2,),
                in_specs=[
                    pl.BlockSpec((sections, pair, padded), lambda i, tile: (0, i, 0)),
                    pl.BlockSpec((padded, columns), lambda i, tile: (0, 0)),
                ],
                out_specs=(
                    pl.BlockSpec((2, sections * UNIT, columns), lambda i, tile: (i, 0, 0)),
                    pl.BlockSpec((2, sections * UNIT, window), lambda i, tile: (i, 0, 0)),
                    pl.BlockSpec((2, sections, LANES), lambda i, tile: (i, 0, 0)),
                ),
            ),
            compiler_params=PARAMS,
            cost_estimate=FREE,
            name=name,
        )(tile.reshape(1), rows, early_weight)

    own_main, own_window, own_notes = forward(from_own, "forward_own")
    other_main, other_window, other_notes = forward(from_other, "forward_other")
    last_window = lax.dynamic_update_slice_in_dim(
        jnp.zeros((window, columns), BF), last, last_row - tile * LANES, 0
    )
    partial = pl.pallas_call(
        tail_kernel,
        out_shape=pltpu.HBM((units, sections * UNIT, columns), BF),
        in_specs=[SMEM] + [VMEM] * 5,
        out_specs=VMEM,
        compiler_params=PARAMS,
        cost_estimate=FREE,
        name="tail",
    )(core_index, own_window, other_window, last_window, own_main, other_main)
    partial = lax.all_to_all(partial, along_first, 0, 0, tiled=True)
    weight = lax.dynamic_update_slice_in_dim(early_weight, last, last_row, 0)

    at = LANES - (padded - chunk)
    table = jnp.where(
        core == 0,
        jnp.concatenate([own_notes, other_notes]),
        jnp.concatenate([other_notes, own_notes]),
    )
    table = jnp.swapaxes(table[:, :, at : at + 3], 0, 1).astype(jnp.int32)
    here = lax.dynamic_slice_in_dim(table, section, 1, 1)[:, 0]
    has = here[:, 1] > 0
    spots = jnp.arange(sections)
    where = fill_places(here[:, 2], has, spots)
    has = has.astype(jnp.int32)

    share = units // tensors
    back = jnp.array([0, 0, 1, 1, -1, -1, 2, 2])
    from_section = (section // 2 - back) % along * 2 + (y_lo ^ jnp.array([0, 1] * 4))
    run = jnp.sum(
        jnp.where(from_section[:, None, None] == spots, table[None, :, :, 0], 0), axis=2
    )
    side = run // share
    pick = (side % 2 == core) * along + spots // 2
    pick = ((pick * 2 + side // 2) * 2 + spots % 2) * share + run % share
    pick = pick.reshape(-1).astype(jnp.int32)
    hat, hat_inv = pl.pallas_call(
        hat_kernel,
        out_shape=(shape((share * UNIT, depth), F32), shape((share * UNIT, LANES), F32)),
        grid_spec=pltpu.PrefetchScalarGridSpec(
            num_scalar_prefetch=1,
            grid=(share,),
            in_specs=[ANY, pl.BlockSpec((UNIT, depth), lambda i, first: (first[0] + i, 0))],
            out_specs=(
                pl.BlockSpec((UNIT, depth), lambda i, first: (i, 0)),
                pl.BlockSpec((UNIT, LANES), lambda i, first: (i, 0)),
            ),
        ),
        compiler_params=WIDE,
        cost_estimate=FREE,
        name="vision_hat",
    )((tensor * share).reshape(1).astype(jnp.int32), table, vision_rows)
    upstream, text_stat = pl.pallas_call(
        prepare_kernel,
        out_shape=(shape((slots, columns), F32), shape((8, LANES), F32)),
        in_specs=[ANY] + [VMEM] * 3,
        out_specs=(VMEM, VMEM),
        compiler_params=PARAMS,
        cost_estimate=FREE,
        name="prepare",
    )(hat_inv, text_rows, out_cotangent, text_gain_row)
    feature, slope, stat = pl.pallas_call(
        slots_kernel,
        out_shape=(
            shape((slots, columns), BF),
            shape((slots, columns), F32),
            shape((8, LANES), F32),
        ),
        in_specs=[SMEM, ANY, ANY, VMEM, VMEM, VMEM],
        out_specs=(VMEM, VMEM, VMEM),
        compiler_params=PARAMS,
        cost_estimate=FREE,
        name="slots",
    )(where, pick, hat_inv, partial, upstream, text_stat)
    stats = [stat] + [
        lax.ppermute(stat, ("y_hi", "core"), [(i, i ^ turn) for i in range(tensors)])
        for turn in range(1, tensors)
    ]
    grads = pl.pallas_call(
        functools.partial(grad_kernel, width),
        out_shape=shape((sections, UNIT, columns), BF),
        in_specs=[SMEM, SMEM] + [VMEM] * (3 + tensors),
        out_specs=VMEM,
        compiler_params=PARAMS,
        cost_estimate=FREE,
        name="grads",
    )(where, has, feature, slope, upstream, *stats)
    def turn(block, dx, dy=0):
        moves = [
            (i, (i // along ^ dy) * along + (i + dx) % along) for i in range(sections)
        ]
        return lax.ppermute(block, ("y_lo", "x"), moves)

    across = turn(grads, 0, 1)
    left, right = lax.optimization_barrier((turn(grads, 1), turn(grads, -1)))
    left_across, right_across = turn(across, 1), turn(across, -1)
    opposite, opposite_across = turn(left, 1), turn(right_across, -1)
    blocks = [grads, across, left, left_across, right, right_across, opposite, opposite_across]
    grads = pl.pallas_call(
        arrange_kernel,
        out_shape=shape((sections * sections, UNIT, columns), BF),
        in_specs=[SMEM] + [VMEM] * sections,
        out_specs=VMEM,
        compiler_params=PARAMS,
        cost_estimate=FREE,
        name="arrange",
    )(pick, *blocks)
    normed = pl.pallas_call(
        functools.partial(normed_kernel, width),
        out_shape=shape((slots, columns), BF),
        in_specs=[SMEM, SMEM] + [VMEM] * (3 + tensors),
        out_specs=VMEM,
        compiler_params=PARAMS,
        cost_estimate=FREE,
        name="normed",
    )(where, has, text_rows, feature, text_gain_row, *stats)

    peers = sections * 2
    quarter = sections * units // 4

    def product(first, count, dtype, name):
        return pl.pallas_call(
            back_kernel,
            out_shape=shape((count * quarter * UNIT, padded), dtype),
            grid=(count,),
            in_specs=[
                pl.BlockSpec((quarter, UNIT, columns), lambda i: (first + i, 0, 0)),
                pl.BlockSpec((padded, columns), lambda i: (0, 0)),
            ],
            out_specs=pl.BlockSpec((quarter * UNIT, padded), lambda i: (i, 0)),
            compiler_params=PARAMS,
            cost_estimate=FREE,
            name=name,
        )(grads, weight)

    got = [
        lax.ppermute(product(h, 1, BF, f"give{h}"), "core", swap_core) for h in range(2)
    ]
    total = pl.pallas_call(
        join_kernel,
        out_shape=pltpu.HBM((peers, share * UNIT, padded), BF),
        grid=(2,),
        in_specs=[pl.BlockSpec((quarter * UNIT, padded), lambda i: (i, 0))]
        + [pl.BlockSpec((quarter * UNIT, padded), lambda i: (0, 0))] * 2,
        out_specs=pl.BlockSpec((sections, share * UNIT, padded), lambda i: (i, 0, 0)),
        compiler_params=PARAMS,
        cost_estimate=FREE,
        name="join",
    )(product(2, 2, F32, "keep"), *got)
    back = lax.all_to_all(total, ("x", "y_hi", "y_lo"), 0, 0, tiled=True)
    order = []
    for y_lo in range(2):
        for x in range(along):
            order.append([(x * 2 + y_hi) * 2 + y_lo for y_hi in range(2)])
    vision_grad = pl.pallas_call(
        functools.partial(final_kernel, chunk, order),
        out_shape=shape((share * UNIT, depth), BF),
        grid=(share,),
        in_specs=[
            pl.BlockSpec((peers, UNIT, padded), lambda i: (0, i, 0)),
            pl.BlockSpec((UNIT, depth), lambda i: (i, 0)),
            pl.BlockSpec((UNIT, LANES), lambda i: (i, 0)),
            pl.BlockSpec((depth,), lambda i: (0,)),
        ],
        out_specs=pl.BlockSpec((UNIT, depth), lambda i: (i, 0)),
        compiler_params=PARAMS,
        cost_estimate=FREE,
        name="vision_back",
    )(back, hat, hat_inv, vision_gain)
    return normed, vision_grad


def solution(mesh):
    mesh = Mesh(
        mesh.devices.reshape(2, mesh.shape["section"] // 2, mesh.shape["dp"], -1, 2),
        ("y_lo", "x", "dp", "y_hi", "core"),
    )
    rows, tensor = ("y_lo", "x", "dp"), ("y_hi", "core")
    in_specs = (
        P(rows, None),
        P(),
        P(),
        P(rows, tensor),
        P(rows, tensor),
        P(tensor),
        P(rows),
        P(rows, tensor),
    )
    out_specs = (P(rows, tensor), P((*rows, *tensor), None))

    def program(*args):
        body = functools.partial(shards, args[4].shape[1])
        return jax.shard_map(
            body, mesh=mesh, in_specs=in_specs, out_specs=out_specs, check_vma=False
        )(*args)

    return program
```

```python
import functools

import jax
import jax.numpy as jnp
from jax import lax
from jax.experimental import pallas as pl
from jax.experimental.pallas import tpu as pltpu
from jax.sharding import Mesh
from jax.sharding import PartitionSpec as P

UNIT = 16
LANES = 128
VISION_EPS = 1e-05
EPSILON = 1e-06
HALF_ROOT = 0.7071067811865476
INV_ROOT_TWO_PI = 0.3989422804014327
BF = jnp.bfloat16
F32 = jnp.float32
VMEM = pl.BlockSpec(memory_space=pltpu.VMEM)
SMEM = pl.BlockSpec(memory_space=pltpu.SMEM)
ANY = pl.BlockSpec(memory_space=pl.ANY)
FREE = pl.CostEstimate(flops=0, transcendentals=0, bytes_accessed=0)
PARAMS = pltpu.CompilerParams(vmem_limit_bytes=40 * 2**20)
WIDE = pltpu.CompilerParams(vmem_limit_bytes=60 * 2**20)
NT = (((1,), (1,)), ((), ()))


def shape(dims, dtype):
    return jax.ShapeDtypeStruct(dims, dtype)


def run_order(slot_ref, units, section_slots, along):
    slots = [slot_ref[u * UNIT] for u in range(units)]
    alive = [slot >= 0 for slot in slots]
    target = [jnp.maximum(slot, 0) // section_slots for slot in slots]
    target = [t % along * 2 + t // along for t in target]
    place = [jnp.where(a, t, -1) for a, t in zip(alive, target)]
    taken = []
    for spot in range(units):
        hits = [jnp.where(p == spot, 1, 0) for p in place]
        taken.append(functools.reduce(lambda a, b: a + b, hits))
    dead_rank = jnp.int32(0)
    for u in range(units):
        free_rank = jnp.int32(0)
        filler = jnp.int32(0)
        for spot in range(units):
            free = 1 - taken[spot]
            filler = jnp.where((free > 0) & (free_rank == dead_rank), spot, filler)
            free_rank = free_rank + free
        place[u] = jnp.where(alive[u], place[u], filler)
        dead_rank = dead_rank + jnp.where(alive[u], 0, 1)
    return slots, alive, place


def norm_kernel(
    chunk, own_slots, section_slots, along, slot_ref, core_ref, rows_ref, gain_ref, bias_ref, out_ref, held, sems
):
    parts, high, padded = out_ref.shape
    half = high // UNIT
    units = 2 * half
    slots, alive, place = run_order(slot_ref, units, section_slots, along)
    notes = []
    for i in range(half):
        run, slot, live = jnp.int32(0), jnp.int32(0), jnp.int32(0)
        for u in range(units):
            here = place[u] == core_ref[0] * half + i
            run = jnp.where(here, u, run)
            slot = jnp.where(here, slots[u], slot)
            live = jnp.where(here & alive[u], 1, live)
        spot = jnp.where(live > 0, slot // UNIT % (own_slots // UNIT), 0)
        notes.append((run, live, spot))
    copies = []
    for i, (run, _, _) in enumerate(notes):
        rows = pl.ds(pl.multiple_of(run * UNIT, UNIT), UNIT)
        copies.append(pltpu.make_async_copy(rows_ref.at[rows], held.at[i], sems.at[i]))
        copies[i].start()
    gain, bias = gain_ref[...].reshape(1, -1), bias_ref[...].reshape(1, -1)
    lane = lax.broadcasted_iota(jnp.int32, (UNIT, padded - chunk), 1)
    for i, (run, live, spot) in enumerate(notes):
        copies[i].wait()
        wide = held[i].astype(F32)
        centered = wide - jnp.mean(wide, axis=1, keepdims=True)
        inv = lax.rsqrt(jnp.mean(centered * centered, axis=1, keepdims=True) + VISION_EPS)
        normed = (centered * inv * gain + bias).astype(BF)
        note = jnp.where(lane == 0, run, jnp.where(lane == 1, live, spot)).astype(F32).astype(BF)
        for k in range(parts):
            at = (k % 2 * (parts // 2) + k // 2) * chunk
            out_ref[k, i * UNIT : (i + 1) * UNIT] = jnp.concatenate(
                [normed[:, at : at + chunk], note], axis=1
            )


def forward_kernel(tile_ref, rows_ref, weight_ref, out_ref, window_ref, note_ref):
    sections, high, depth = rows_ref.shape
    at = pl.ds(pl.multiple_of(tile_ref[0] * LANES, LANES), window_ref.shape[2])
    product = jnp.dot(
        rows_ref[...].reshape(sections * high, depth), weight_ref[...], preferred_element_type=F32
    )
    product = product.reshape(sections, high, product.shape[1])
    for j in range(high // UNIT):
        run = slice(j * UNIT, (j + 1) * UNIT)
        out_ref[j] = product[:, run].reshape(sections * UNIT, -1)
        window_ref[j] = rows_ref[:, run, at].reshape(sections * UNIT, -1)
        heads = [rows_ref[s, run, depth - LANES :][:1] for s in range(sections)]
        note_ref[j] = jnp.concatenate([head.astype(F32) for head in heads], axis=0)


def tail_kernel(core_ref, own_window_ref, other_window_ref, weight_ref, own_ref, other_ref, out_ref):
    half = own_ref.shape[0]
    halves = ((core_ref[0], own_window_ref, own_ref), (1 - core_ref[0], other_window_ref, other_ref))
    for side, window_ref, main_ref in halves:
        for j in range(half):
            product = jnp.dot(window_ref[j], weight_ref[...], preferred_element_type=F32)
            out_ref[side * half + j] = (main_ref[j] + product).astype(BF)


def prepare_kernel(text_ref, cot_ref, gain_ref, upstream_ref, stat_ref):
    upstream_ref[...] = cot_ref[...].astype(F32) * gain_ref[...]
    text = text_ref[...].astype(F32)
    square = jnp.sum(text * text, axis=1, keepdims=True)
    square = jnp.broadcast_to(square, (square.shape[0], LANES))
    stat_ref[...] = jnp.transpose(square)[: stat_ref.shape[0]]


def slots_kernel(
    place_ref, parts_ref, upstream_ref, text_stat_ref, feature_ref, slope_ref, grad_ref, stat_ref, held, sem
):
    copy = pltpu.make_async_copy(upstream_ref, held, sem)
    copy.start()
    runs = feature_ref.shape[0] // UNIT
    for s in range(runs):
        rows = slice(s * UNIT, (s + 1) * UNIT)
        projected = parts_ref[0, rows].astype(F32)
        for k in range(1, parts_ref.shape[0]):
            projected = projected + parts_ref[k, rows].astype(F32)
        gate = 0.5 * (1.0 + lax.erf(projected * HALF_ROOT))
        feature_ref[rows] = (projected * gate).astype(BF)
        slope_ref[rows] = gate + projected * jnp.exp(-0.5 * projected * projected) * INV_ROOT_TWO_PI
    copy.wait()
    lane = lax.broadcasted_iota(jnp.int32, (UNIT, LANES), 1)
    stats = []
    for s in range(runs):
        rows = slice(s * UNIT, (s + 1) * UNIT)
        at = pl.ds(pl.multiple_of(place_ref[s] * UNIT, UNIT), UNIT)
        wide, upstream = feature_ref[rows].astype(F32), held[at]
        grad_ref[rows] = upstream
        square = jnp.sum(wide * wide, axis=1, keepdims=True)
        cross = jnp.sum(upstream * wide, axis=1, keepdims=True)
        stats.append(jnp.where(lane == 0, square, cross))
    stat = jnp.transpose(jnp.concatenate(stats, axis=0))[: stat_ref.shape[0]]
    row = lax.broadcasted_iota(jnp.int32, stat.shape, 0)
    stat_ref[...] = jnp.where(row == 2, text_stat_ref[...], stat)


def row_scales(stat_refs, width):
    stat = sum(ref[...] for ref in stat_refs) / width
    pad = jnp.zeros((LANES - stat.shape[0], LANES), F32)
    return jnp.transpose(jnp.concatenate([stat, pad], axis=0))


def grad_kernel(
    width, live_ref, feature_ref, slope_ref, upstream_ref, *refs
):
    stat_refs, grad_ref = refs[:-1], refs[-1]
    stat = row_scales(stat_refs, width)
    for s in range(feature_ref.shape[0] // UNIT):
        rows = slice(s * UNIT, (s + 1) * UNIT)
        inv, cross = lax.rsqrt(stat[rows, 0:1] + EPSILON), stat[rows, 1:2]
        wide = feature_ref[rows].astype(F32)
        hidden_grad = (inv * (upstream_ref[rows] - wide * inv * inv * cross)).astype(BF)
        grad = (hidden_grad.astype(F32) * slope_ref[rows]).astype(BF)
        grad = jnp.where(live_ref[s] > 0, grad, jnp.zeros_like(grad))
        grad_ref[s] = grad


def normed_kernel(
    width, place_ref, live_ref, text_ref, feature_ref, gain_ref, *refs
):
    stat_refs, normed_ref = refs[:-1], refs[-1]
    stat = row_scales(stat_refs, width)
    inv = lax.rsqrt(stat[:, 2:3] + EPSILON)
    normed_ref[...] = (text_ref[...].astype(F32) * inv * gain_ref[...]).astype(BF)
    for s in range(feature_ref.shape[0] // UNIT):
        rows = slice(s * UNIT, (s + 1) * UNIT)
        at = pl.ds(pl.multiple_of(place_ref[s] * UNIT, UNIT), UNIT)

        @pl.when(live_ref[s] > 0)
        def _(rows=rows, at=at):
            inv = lax.rsqrt(stat[rows, 0:1] + EPSILON)
            normed_ref[at] = (feature_ref[rows].astype(F32) * inv * gain_ref[...]).astype(BF)


def arrange_kernel(pick_ref, *refs):
    blocks, out_ref = refs[:-1], refs[-1]
    for b, ref in enumerate(blocks):
        for s in range(ref.shape[0]):
            out_ref[pick_ref[b * ref.shape[0] + s]] = ref[s]


def back_kernel(grads_ref, weight_ref, out_ref):
    grad = grads_ref[...].reshape(out_ref.shape[0], -1)
    product = lax.dot_general(grad, weight_ref[...], NT, preferred_element_type=F32)
    out_ref[...] = product.astype(out_ref.dtype)


def join_kernel(own_ref, low_ref, high_ref, out_ref):
    got = jnp.where(pl.program_id(0) == 0, low_ref[...], high_ref[...])
    total = (own_ref[...] + got.astype(F32)).astype(BF)
    targets, share, _ = out_ref.shape
    for j in range(targets):
        out_ref[j] = total[j * share : (j + 1) * share]


def hat_kernel(first_ref, table_ref, rows_ref, hat_ref, inv_ref):
    del table_ref
    wide = rows_ref[...].astype(F32)
    centered = wide - jnp.mean(wide, axis=1, keepdims=True)
    inv = lax.rsqrt(jnp.mean(centered * centered, axis=1, keepdims=True) + VISION_EPS)
    hat_ref[...] = centered * inv
    inv_ref[...] = jnp.broadcast_to(inv, inv_ref.shape)


def final_kernel(chunk, order, parts_ref, hat_ref, inv_ref, gain_ref, out_ref):
    grad = jnp.concatenate(
        [
            parts_ref[a][:, :chunk].astype(F32) + parts_ref[b][:, :chunk].astype(F32)
            for a, b in order
        ],
        axis=1,
    )
    hat, inv = hat_ref[...], inv_ref[:, 0:1]
    weighted = grad * gain_ref[...].reshape(1, -1)
    weighted_mean = jnp.mean(weighted, axis=1, keepdims=True)
    cross = jnp.mean(weighted * hat, axis=1, keepdims=True)
    out_ref[...] = (inv * (weighted - weighted_mean - hat * cross)).astype(BF)


def ring_gather(block, rows, beside):
    groups = lax.axis_size("dp")
    me = lax.axis_index("dp")
    height = block.shape[0]
    turn = 1 - 2 * lax.axis_index("core")
    ring = ("dp", "core")
    up = [
        (i * 2 + core, (i + 1 - 2 * core) % groups * 2 + core)
        for i in range(groups)
        for core in range(2)
    ]
    down = [(target, source) for source, target in up]
    out = jnp.zeros((rows, block.shape[1]), block.dtype)

    def put(out, piece, owner):
        return lax.dynamic_update_slice_in_dim(out, piece, owner % groups * height, 0)

    out = put(out, block, me)
    rising = falling = block
    for hop in range(1, (groups - 1) // 2 + 1):
        rising = lax.ppermute(rising, ring, up)
        falling = lax.ppermute(falling, ring, down)
        out, rising, falling = lax.optimization_barrier((out, rising, falling))
        if hop == 1:
            rising, falling, beside = lax.optimization_barrier((rising, falling, beside))
        out = put(out, rising, me - hop * turn + groups)
        out = put(out, falling, me + hop * turn + groups)
    last = lax.ppermute(rising, ring, up)
    owner = (me + groups // 2) % groups
    return out, last, owner * height, rising, falling, beside


def after(value, *marks):
    return lax.optimization_barrier((value, marks))[0]


def fill_places(wanted, alive, places):
    taken = jnp.any((wanted[..., :, None] == places) & alive[..., :, None], axis=-2)
    free_rank = jnp.cumsum(~taken, axis=-1) - 1
    dead_rank = jnp.cumsum(~alive, axis=-1) - 1
    fits = (~taken)[..., None, :] & (free_rank[..., None, :] == dead_rank[..., :, None])
    filler = jnp.sum(jnp.where(fits, places, 0), axis=-1)
    return jnp.where(alive, wanted, filler).astype(jnp.int32)


def inverse(place, places):
    return jnp.sum(
        jnp.where(place[..., :, None] == places, places[:, None], 0), axis=-2
    ).astype(jnp.int32)


def shards(
    width, vision_rows, vision_gain, vision_bias, proj_weight, text_rows, text_gain, slot_of_row, out_cotangent
):
    along = lax.axis_size("x")
    sections = 2 * along
    along_first = ("x", "y_lo")
    groups = lax.axis_size("dp")
    tensors = 2 * lax.axis_size("y_hi")
    rows, depth = vision_rows.shape
    slots, columns = text_rows.shape
    units = rows // UNIT
    chunk = depth // sections
    padded = -(-(chunk + 3) // LANES) * LANES
    y_lo = lax.axis_index("y_lo")
    section = lax.axis_index("x") * 2 + y_lo
    core = lax.axis_index("core")
    tensor = lax.axis_index("y_hi") * 2 + core
    places = jnp.arange(units)
    swap_core = [(0, 1), (1, 0)]

    text_gain_row = text_gain.reshape(1, columns)

    half = units // 2
    core_index = core.reshape(1).astype(jnp.int32)
    sent = pl.pallas_call(
        functools.partial(norm_kernel, chunk, slots, slots * groups, along),
        out_shape=pltpu.HBM((sections, half * UNIT, padded), BF),
        in_specs=[SMEM, SMEM, ANY, VMEM, VMEM],
        out_specs=VMEM,
        scratch_shapes=[pltpu.VMEM((half, UNIT, depth), BF), pltpu.SemaphoreType.DMA((half,))],
        compiler_params=WIDE,
        cost_estimate=FREE,
        name="vision_norm",
    )(slot_of_row, core_index, vision_rows, vision_gain, vision_bias)
    early_weight, last, last_row, rising, falling, sent = ring_gather(proj_weight, padded, sent)
    from_own = lax.all_to_all(sent, along_first, 0, 0, tiled=True)
    from_own, *_ = lax.optimization_barrier((from_own, rising, falling))
    from_other = lax.ppermute(from_own, "core", swap_core)

    pair = 2 * UNIT
    height = last.shape[0]
    window = -(-(height + LANES - 8) // LANES) * LANES
    tile = jnp.minimum(last_row // LANES, (padded - window) // LANES).astype(jnp.int32)

    def forward(rows, name):
        return pl.pallas_call(
            forward_kernel,
            out_shape=(
                shape((half, sections * UNIT, columns), F32),
                shape((half, sections * UNIT, window), BF),
                shape((half, sections, LANES), F32),
            ),
            grid_spec=pltpu.PrefetchScalarGridSpec(
                num_scalar_prefetch=1,
                grid=(half // 2,),
                in_specs=[
                    pl.BlockSpec((sections, pair, padded), lambda i, tile: (0, i, 0)),
                    pl.BlockSpec((padded, columns), lambda i, tile: (0, 0)),
                ],
                out_specs=(
                    pl.BlockSpec((2, sections * UNIT, columns), lambda i, tile: (i, 0, 0)),
                    pl.BlockSpec((2, sections * UNIT, window), lambda i, tile: (i, 0, 0)),
                    pl.BlockSpec((2, sections, LANES), lambda i, tile: (i, 0, 0)),
                ),
            ),
            compiler_params=PARAMS,
            cost_estimate=FREE,
            name=name,
        )(tile.reshape(1), rows, early_weight)

    own_main, own_window, own_notes = forward(from_own, "forward_own")
    other_main, other_window, other_notes = forward(from_other, "forward_other")
    last_window = lax.dynamic_update_slice_in_dim(
        jnp.zeros((window, columns), BF), last, last_row - tile * LANES, 0
    )
    partial = pl.pallas_call(
        tail_kernel,
        out_shape=pltpu.HBM((units, sections * UNIT, columns), BF),
        in_specs=[SMEM] + [VMEM] * 5,
        out_specs=VMEM,
        compiler_params=PARAMS,
        cost_estimate=FREE,
        name="tail",
    )(core_index, own_window, other_window, last_window, own_main, other_main)
    partial = lax.all_to_all(partial, along_first, 0, 0, tiled=True)
    weight = lax.dynamic_update_slice_in_dim(early_weight, last, last_row, 0)

    at = LANES - (padded - chunk)
    table = jnp.where(
        core == 0,
        jnp.concatenate([own_notes, other_notes]),
        jnp.concatenate([other_notes, own_notes]),
    )
    table = jnp.swapaxes(table[:, :, at : at + 3], 0, 1).astype(jnp.int32)
    here = lax.dynamic_slice_in_dim(table, section, 1, 1)[:, 0]
    has = here[:, 1] > 0
    spots = jnp.arange(sections)
    where = fill_places(here[:, 2], has, spots)
    has = has.astype(jnp.int32)

    share = units // tensors
    back = jnp.array([0, 0, 1, 1, -1, -1, 2, 2])
    from_section = (section // 2 - back) % along * 2 + (y_lo ^ jnp.array([0, 1] * 4))
    run = jnp.sum(
        jnp.where(from_section[:, None, None] == spots, table[None, :, :, 0], 0), axis=2
    )
    side = run // share
    pick = (side % 2 == core) * along + spots // 2
    pick = ((pick * 2 + side // 2) * 2 + spots % 2) * share + run % share
    pick = pick.reshape(-1).astype(jnp.int32)
    hat, hat_inv = pl.pallas_call(
        hat_kernel,
        out_shape=(shape((share * UNIT, depth), F32), shape((share * UNIT, LANES), F32)),
        grid_spec=pltpu.PrefetchScalarGridSpec(
            num_scalar_prefetch=1,
            grid=(share,),
            in_specs=[ANY, pl.BlockSpec((UNIT, depth), lambda i, first: (first[0] + i, 0))],
            out_specs=(
                pl.BlockSpec((UNIT, depth), lambda i, first: (i, 0)),
                pl.BlockSpec((UNIT, LANES), lambda i, first: (i, 0)),
            ),
        ),
        compiler_params=WIDE,
        cost_estimate=FREE,
        name="vision_hat",
    )((tensor * share).reshape(1).astype(jnp.int32), table, vision_rows)
    upstream, text_stat = pl.pallas_call(
        prepare_kernel,
        out_shape=(pltpu.HBM((slots, columns), F32), shape((8, LANES), F32)),
        in_specs=[VMEM] * 3,
        out_specs=(VMEM, VMEM),
        compiler_params=PARAMS,
        cost_estimate=FREE,
        name="prepare",
    )(text_rows, out_cotangent, after(text_gain_row, hat_inv))
    feature, slope, run_upstream, stat = pl.pallas_call(
        slots_kernel,
        out_shape=(
            shape((slots, columns), BF),
            shape((slots, columns), F32),
            shape((slots, columns), F32),
            shape((8, LANES), F32),
        ),
        in_specs=[SMEM, VMEM, pl.BlockSpec(memory_space=pltpu.HBM), VMEM],
        out_specs=(VMEM,) * 4,
        scratch_shapes=[pltpu.VMEM((slots, columns), F32), pltpu.SemaphoreType.DMA],
        compiler_params=PARAMS,
        cost_estimate=FREE,
        name="slots",
    )(after(where, pick, hat_inv), partial, upstream, text_stat)
    stats = [stat] + [
        lax.ppermute(stat, ("y_hi", "core"), [(i, i ^ turn) for i in range(tensors)])
        for turn in range(1, tensors)
    ]
    grads = pl.pallas_call(
        functools.partial(grad_kernel, width),
        out_shape=shape((sections, UNIT, columns), BF),
        in_specs=[SMEM] + [VMEM] * (3 + tensors),
        out_specs=VMEM,
        compiler_params=PARAMS,
        cost_estimate=FREE,
        name="grads",
    )(has, feature, slope, run_upstream, *stats)
    def turn(block, dx, dy=0):
        moves = [
            (i, (i // along ^ dy) * along + (i + dx) % along) for i in range(sections)
        ]
        return lax.ppermute(block, ("y_lo", "x"), moves)

    across = turn(grads, 0, 1)
    left, right = lax.optimization_barrier((turn(grads, 1), turn(grads, -1)))
    left_across, right_across = turn(across, 1), turn(across, -1)
    opposite, opposite_across = turn(left, 1), turn(right_across, -1)
    blocks = [grads, across, left, left_across, right, right_across, opposite, opposite_across]
    grads = pl.pallas_call(
        arrange_kernel,
        out_shape=shape((sections * sections, UNIT, columns), BF),
        in_specs=[SMEM] + [VMEM] * sections,
        out_specs=VMEM,
        compiler_params=PARAMS,
        cost_estimate=FREE,
        name="arrange",
    )(pick, *blocks)
    normed = pl.pallas_call(
        functools.partial(normed_kernel, width),
        out_shape=shape((slots, columns), BF),
        in_specs=[SMEM, SMEM] + [VMEM] * (3 + tensors),
        out_specs=VMEM,
        compiler_params=PARAMS,
        cost_estimate=FREE,
        name="normed",
    )(where, has, text_rows, feature, text_gain_row, *stats)

    peers = sections * 2
    quarter = sections * units // 4

    def product(first, count, dtype, name):
        return pl.pallas_call(
            back_kernel,
            out_shape=shape((count * quarter * UNIT, padded), dtype),
            grid=(count,),
            in_specs=[
                pl.BlockSpec((quarter, UNIT, columns), lambda i: (first + i, 0, 0)),
                pl.BlockSpec((padded, columns), lambda i: (0, 0)),
            ],
            out_specs=pl.BlockSpec((quarter * UNIT, padded), lambda i: (i, 0)),
            compiler_params=PARAMS,
            cost_estimate=FREE,
            name=name,
        )(grads, weight)

    got = [
        lax.ppermute(product(h, 1, BF, f"give{h}"), "core", swap_core) for h in range(2)
    ]
    total = pl.pallas_call(
        join_kernel,
        out_shape=pltpu.HBM((peers, share * UNIT, padded), BF),
        grid=(2,),
        in_specs=[pl.BlockSpec((quarter * UNIT, padded), lambda i: (i, 0))]
        + [pl.BlockSpec((quarter * UNIT, padded), lambda i: (0, 0))] * 2,
        out_specs=pl.BlockSpec((sections, share * UNIT, padded), lambda i: (i, 0, 0)),
        compiler_params=PARAMS,
        cost_estimate=FREE,
        name="join",
    )(product(2, 2, F32, "keep"), *got)
    back = lax.all_to_all(total, ("x", "y_hi", "y_lo"), 0, 0, tiled=True)
    order = []
    for y_lo in range(2):
        for x in range(along):
            order.append([(x * 2 + y_hi) * 2 + y_lo for y_hi in range(2)])
    vision_grad = pl.pallas_call(
        functools.partial(final_kernel, chunk, order),
        out_shape=shape((share * UNIT, depth), BF),
        grid=(share,),
        in_specs=[
            pl.BlockSpec((peers, UNIT, padded), lambda i: (0, i, 0)),
            pl.BlockSpec((UNIT, depth), lambda i: (i, 0)),
            pl.BlockSpec((UNIT, LANES), lambda i: (i, 0)),
            pl.BlockSpec((depth,), lambda i: (0,)),
        ],
        out_specs=pl.BlockSpec((UNIT, depth), lambda i: (i, 0)),
        compiler_params=PARAMS,
        cost_estimate=FREE,
        name="vision_back",
    )(back, hat, hat_inv, vision_gain)
    return normed, vision_grad


def solution(mesh):
    mesh = Mesh(
        mesh.devices.reshape(2, mesh.shape["section"] // 2, mesh.shape["dp"], -1, 2),
        ("y_lo", "x", "dp", "y_hi", "core"),
    )
    rows, tensor = ("y_lo", "x", "dp"), ("y_hi", "core")
    in_specs = (
        P(rows, None),
        P(),
        P(),
        P(rows, tensor),
        P(rows, tensor),
        P(tensor),
        P(rows),
        P(rows, tensor),
    )
    out_specs = (P(rows, tensor), P((*rows, *tensor), None))

    def program(*args):
        body = functools.partial(shards, args[4].shape[1])
        return jax.shard_map(
            body, mesh=mesh, in_specs=in_specs, out_specs=out_specs, check_vma=False
        )(*args)

    return program
```

```python
import functools

import jax
import jax.numpy as jnp
from jax import lax
from jax.experimental import pallas as pl
from jax.experimental.pallas import tpu as pltpu
from jax.sharding import Mesh
from jax.sharding import PartitionSpec as P

UNIT = 16
LANES = 128
VISION_EPS = 1e-05
EPSILON = 1e-06
HALF_ROOT = 0.7071067811865476
INV_ROOT_TWO_PI = 0.3989422804014327
BF = jnp.bfloat16
F32 = jnp.float32
VMEM = pl.BlockSpec(memory_space=pltpu.VMEM)
SMEM = pl.BlockSpec(memory_space=pltpu.SMEM)
ANY = pl.BlockSpec(memory_space=pl.ANY)
FREE = pl.CostEstimate(flops=0, transcendentals=0, bytes_accessed=0)
PARAMS = pltpu.CompilerParams(vmem_limit_bytes=40 * 2**20)
WIDE = pltpu.CompilerParams(vmem_limit_bytes=60 * 2**20)
NT = (((1,), (1,)), ((), ()))


def shape(dims, dtype):
    return jax.ShapeDtypeStruct(dims, dtype)


def run_order(slot_ref, units, section_slots, along):
    slots = [slot_ref[u * UNIT] for u in range(units)]
    alive = [slot >= 0 for slot in slots]
    target = [jnp.maximum(slot, 0) // section_slots for slot in slots]
    target = [t % along * 2 + t // along for t in target]
    place = [jnp.where(a, t, -1) for a, t in zip(alive, target)]
    taken = []
    for spot in range(units):
        hits = [jnp.where(p == spot, 1, 0) for p in place]
        taken.append(functools.reduce(lambda a, b: a + b, hits))
    dead_rank = jnp.int32(0)
    for u in range(units):
        free_rank = jnp.int32(0)
        filler = jnp.int32(0)
        for spot in range(units):
            free = 1 - taken[spot]
            filler = jnp.where((free > 0) & (free_rank == dead_rank), spot, filler)
            free_rank = free_rank + free
        place[u] = jnp.where(alive[u], place[u], filler)
        dead_rank = dead_rank + jnp.where(alive[u], 0, 1)
    return slots, alive, place


def norm_kernel(
    chunk, own_slots, section_slots, along, slot_ref, core_ref, rows_ref, gain_ref, bias_ref, out_ref, held, made, sems, out_sems
):
    parts, high, padded = out_ref.shape
    half = high // UNIT
    units = 2 * half
    slots, alive, place = run_order(slot_ref, units, section_slots, along)
    notes = []
    for i in range(half):
        run, slot, live = jnp.int32(0), jnp.int32(0), jnp.int32(0)
        for u in range(units):
            here = place[u] == core_ref[0] * half + i
            run = jnp.where(here, u, run)
            slot = jnp.where(here, slots[u], slot)
            live = jnp.where(here & alive[u], 1, live)
        spot = jnp.where(live > 0, slot // UNIT % (own_slots // UNIT), 0)
        notes.append((run, live, spot))
    copies = []
    for i, (run, _, _) in enumerate(notes):
        rows = pl.ds(pl.multiple_of(run * UNIT, UNIT), UNIT)
        copies.append(pltpu.make_async_copy(rows_ref.at[rows], held.at[i], sems.at[i]))
        copies[i].start()
    gain, bias = gain_ref[...].reshape(1, -1), bias_ref[...].reshape(1, -1)
    lane = lax.broadcasted_iota(jnp.int32, (UNIT, padded - chunk), 1)
    for i, (run, live, spot) in enumerate(notes):
        copies[i].wait()
        wide = held[i].astype(F32)
        centered = wide - jnp.mean(wide, axis=1, keepdims=True)
        inv = lax.rsqrt(jnp.mean(centered * centered, axis=1, keepdims=True) + VISION_EPS)
        normed = (centered * inv * gain + bias).astype(BF)
        note = jnp.where(lane == 0, run, jnp.where(lane == 1, live, spot)).astype(F32).astype(BF)
        for k in range(parts):
            at = (k % 2 * (parts // 2) + k // 2) * chunk
            made[i, k] = jnp.concatenate([normed[:, at : at + chunk], note], axis=1)
        target = out_ref.at[:, pl.ds(i * UNIT, UNIT)]
        copies.append(pltpu.make_async_copy(made.at[i], target, out_sems.at[i]))
        copies[-1].start()
    for copy in copies[half:]:
        copy.wait()


def forward_kernel(tile_ref, rows_ref, weight_ref, out_ref, window_ref, note_ref):
    sections, high, depth = rows_ref.shape
    at = pl.ds(pl.multiple_of(tile_ref[0] * LANES, LANES), window_ref.shape[2])
    product = jnp.dot(
        rows_ref[...].reshape(sections * high, depth), weight_ref[...], preferred_element_type=F32
    )
    product = product.reshape(sections, high, product.shape[1])
    for j in range(high // UNIT):
        run = slice(j * UNIT, (j + 1) * UNIT)
        out_ref[j] = product[:, run].reshape(sections * UNIT, -1)
        window_ref[j] = rows_ref[:, run, at].reshape(sections * UNIT, -1)
        heads = [rows_ref[s, run, depth - LANES :][:1] for s in range(sections)]
        note_ref[j] = jnp.concatenate([head.astype(F32) for head in heads], axis=0)


def tail_kernel(
    core_ref, own_window_ref, other_window_ref, weight_ref, own_ref, other_ref, out_ref, made, sems
):
    half = own_ref.shape[0]
    halves = ((core_ref[0], own_window_ref, own_ref), (1 - core_ref[0], other_window_ref, other_ref))
    copies = []
    for side, window_ref, main_ref in halves:
        for j in range(half):
            n = len(copies)
            product = jnp.dot(window_ref[j], weight_ref[...], preferred_element_type=F32)
            made[n] = (main_ref[j] + product).astype(BF)
            target = out_ref.at[side * half + j]
            copies.append(pltpu.make_async_copy(made.at[n], target, sems.at[n]))
            copies[n].start()
    for copy in copies:
        copy.wait()


def prepare_kernel(text_ref, cot_ref, gain_ref, upstream_ref, stat_ref):
    upstream_ref[...] = cot_ref[...].astype(F32) * gain_ref[...]
    text = text_ref[...].astype(F32)
    square = jnp.sum(text * text, axis=1, keepdims=True)
    square = jnp.broadcast_to(square, (square.shape[0], LANES))
    stat_ref[...] = jnp.transpose(square)[: stat_ref.shape[0]]


def slots_kernel(
    place_ref, parts_ref, upstream_ref, text_stat_ref, feature_ref, slope_ref, grad_ref, stat_ref, held, sem
):
    copy = pltpu.make_async_copy(upstream_ref, held, sem)
    copy.start()
    runs = feature_ref.shape[0] // UNIT
    for s in range(runs):
        rows = slice(s * UNIT, (s + 1) * UNIT)
        projected = parts_ref[0, rows].astype(F32)
        for k in range(1, parts_ref.shape[0]):
            projected = projected + parts_ref[k, rows].astype(F32)
        gate = 0.5 * (1.0 + lax.erf(projected * HALF_ROOT))
        feature_ref[rows] = (projected * gate).astype(BF)
        slope_ref[rows] = gate + projected * jnp.exp(-0.5 * projected * projected) * INV_ROOT_TWO_PI
    copy.wait()
    lane = lax.broadcasted_iota(jnp.int32, (UNIT, LANES), 1)
    stats = []
    for s in range(runs):
        rows = slice(s * UNIT, (s + 1) * UNIT)
        at = pl.ds(pl.multiple_of(place_ref[s] * UNIT, UNIT), UNIT)
        wide, upstream = feature_ref[rows].astype(F32), held[at]
        grad_ref[rows] = upstream
        square = jnp.sum(wide * wide, axis=1, keepdims=True)
        cross = jnp.sum(upstream * wide, axis=1, keepdims=True)
        stats.append(jnp.where(lane == 0, square, cross))
    stat = jnp.transpose(jnp.concatenate(stats, axis=0))[: stat_ref.shape[0]]
    row = lax.broadcasted_iota(jnp.int32, stat.shape, 0)
    stat_ref[...] = jnp.where(row == 2, text_stat_ref[...], stat)


def row_scales(stat_refs, width):
    stat = sum(ref[...] for ref in stat_refs) / width
    pad = jnp.zeros((LANES - stat.shape[0], LANES), F32)
    return jnp.transpose(jnp.concatenate([stat, pad], axis=0))


def grad_kernel(
    width, live_ref, feature_ref, slope_ref, upstream_ref, *refs
):
    stat_refs, grad_ref = refs[:-1], refs[-1]
    stat = row_scales(stat_refs, width)
    for s in range(feature_ref.shape[0] // UNIT):
        rows = slice(s * UNIT, (s + 1) * UNIT)
        inv, cross = lax.rsqrt(stat[rows, 0:1] + EPSILON), stat[rows, 1:2]
        wide = feature_ref[rows].astype(F32)
        hidden_grad = (inv * (upstream_ref[rows] - wide * inv * inv * cross)).astype(BF)
        grad = (hidden_grad.astype(F32) * slope_ref[rows]).astype(BF)
        grad = jnp.where(live_ref[s] > 0, grad, jnp.zeros_like(grad))
        grad_ref[s] = grad


def normed_kernel(
    width, place_ref, live_ref, text_ref, feature_ref, gain_ref, *refs
):
    stat_refs, normed_ref = refs[:-1], refs[-1]
    stat = row_scales(stat_refs, width)
    inv = lax.rsqrt(stat[:, 2:3] + EPSILON)
    normed_ref[...] = (text_ref[...].astype(F32) * inv * gain_ref[...]).astype(BF)
    for s in range(feature_ref.shape[0] // UNIT):
        rows = slice(s * UNIT, (s + 1) * UNIT)
        at = pl.ds(pl.multiple_of(place_ref[s] * UNIT, UNIT), UNIT)

        @pl.when(live_ref[s] > 0)
        def _(rows=rows, at=at):
            inv = lax.rsqrt(stat[rows, 0:1] + EPSILON)
            normed_ref[at] = (feature_ref[rows].astype(F32) * inv * gain_ref[...]).astype(BF)


def arrange_kernel(pick_ref, *refs):
    blocks, out_ref = refs[:-1], refs[-1]
    for b, ref in enumerate(blocks):
        for s in range(ref.shape[0]):
            out_ref[pick_ref[b * ref.shape[0] + s]] = ref[s]


def back_kernel(grads_ref, weight_ref, out_ref):
    grad = grads_ref[...].reshape(out_ref.shape[0], -1)
    product = lax.dot_general(grad, weight_ref[...], NT, preferred_element_type=F32)
    out_ref[...] = product.astype(out_ref.dtype)


def join_kernel(own_ref, low_ref, high_ref, out_ref):
    got = jnp.where(pl.program_id(0) == 0, low_ref[...], high_ref[...])
    total = (own_ref[...] + got.astype(F32)).astype(BF)
    targets, share, _ = out_ref.shape
    for j in range(targets):
        out_ref[j] = total[j * share : (j + 1) * share]


def hat_kernel(first_ref, table_ref, rows_ref, hat_ref, inv_ref):
    del table_ref
    wide = rows_ref[...].astype(F32)
    centered = wide - jnp.mean(wide, axis=1, keepdims=True)
    inv = lax.rsqrt(jnp.mean(centered * centered, axis=1, keepdims=True) + VISION_EPS)
    hat_ref[...] = centered * inv
    inv_ref[...] = jnp.broadcast_to(inv, inv_ref.shape)


def final_kernel(chunk, order, parts_ref, hat_ref, inv_ref, gain_ref, out_ref):
    grad = jnp.concatenate(
        [
            parts_ref[a][:, :chunk].astype(F32) + parts_ref[b][:, :chunk].astype(F32)
            for a, b in order
        ],
        axis=1,
    )
    hat, inv = hat_ref[...], inv_ref[:, 0:1]
    weighted = grad * gain_ref[...].reshape(1, -1)
    weighted_mean = jnp.mean(weighted, axis=1, keepdims=True)
    cross = jnp.mean(weighted * hat, axis=1, keepdims=True)
    out_ref[...] = (inv * (weighted - weighted_mean - hat * cross)).astype(BF)


def ring_gather(block, rows, beside):
    groups = lax.axis_size("dp")
    me = lax.axis_index("dp")
    height = block.shape[0]
    turn = 1 - 2 * lax.axis_index("core")
    ring = ("dp", "core")
    up = [
        (i * 2 + core, (i + 1 - 2 * core) % groups * 2 + core)
        for i in range(groups)
        for core in range(2)
    ]
    down = [(target, source) for source, target in up]
    out = jnp.zeros((rows, block.shape[1]), block.dtype)

    def put(out, piece, owner):
        return lax.dynamic_update_slice_in_dim(out, piece, owner % groups * height, 0)

    out = put(out, block, me)
    rising = falling = block
    for hop in range(1, (groups - 1) // 2 + 1):
        rising = lax.ppermute(rising, ring, up)
        falling = lax.ppermute(falling, ring, down)
        out, rising, falling = lax.optimization_barrier((out, rising, falling))
        if hop == 1:
            rising, falling, beside = lax.optimization_barrier((rising, falling, beside))
        out = put(out, rising, me - hop * turn + groups)
        out = put(out, falling, me + hop * turn + groups)
    last = lax.ppermute(rising, ring, up)
    owner = (me + groups // 2) % groups
    return out, last, owner * height, rising, falling, beside


def after(value, *marks):
    return lax.optimization_barrier((value, marks))[0]


def fill_places(wanted, alive, places):
    taken = jnp.any((wanted[..., :, None] == places) & alive[..., :, None], axis=-2)
    free_rank = jnp.cumsum(~taken, axis=-1) - 1
    dead_rank = jnp.cumsum(~alive, axis=-1) - 1
    fits = (~taken)[..., None, :] & (free_rank[..., None, :] == dead_rank[..., :, None])
    filler = jnp.sum(jnp.where(fits, places, 0), axis=-1)
    return jnp.where(alive, wanted, filler).astype(jnp.int32)


def inverse(place, places):
    return jnp.sum(
        jnp.where(place[..., :, None] == places, places[:, None], 0), axis=-2
    ).astype(jnp.int32)


def shards(
    width, vision_rows, vision_gain, vision_bias, proj_weight, text_rows, text_gain, slot_of_row, out_cotangent
):
    along = lax.axis_size("x")
    sections = 2 * along
    along_first = ("x", "y_lo")
    groups = lax.axis_size("dp")
    tensors = 2 * lax.axis_size("y_hi")
    rows, depth = vision_rows.shape
    slots, columns = text_rows.shape
    units = rows // UNIT
    chunk = depth // sections
    padded = -(-(chunk + 3) // LANES) * LANES
    y_lo = lax.axis_index("y_lo")
    section = lax.axis_index("x") * 2 + y_lo
    core = lax.axis_index("core")
    tensor = lax.axis_index("y_hi") * 2 + core
    places = jnp.arange(units)
    swap_core = [(0, 1), (1, 0)]

    text_gain_row = text_gain.reshape(1, columns)

    half = units // 2
    core_index = core.reshape(1).astype(jnp.int32)
    sent = pl.pallas_call(
        functools.partial(norm_kernel, chunk, slots, slots * groups, along),
        out_shape=pltpu.HBM((sections, half * UNIT, padded), BF),
        in_specs=[SMEM, SMEM, ANY, VMEM, VMEM],
        out_specs=ANY,
        scratch_shapes=[
            pltpu.VMEM((half, UNIT, depth), BF),
            pltpu.VMEM((half, sections, UNIT, padded), BF),
            pltpu.SemaphoreType.DMA((half,)),
            pltpu.SemaphoreType.DMA((half,)),
        ],
        compiler_params=WIDE,
        cost_estimate=FREE,
        name="vision_norm",
    )(slot_of_row, core_index, vision_rows, vision_gain, vision_bias)
    early_weight, last, last_row, rising, falling, sent = ring_gather(proj_weight, padded, sent)
    from_own = lax.all_to_all(sent, along_first, 0, 0, tiled=True)
    from_own, *_ = lax.optimization_barrier((from_own, rising, falling))
    from_other = lax.ppermute(from_own, "core", swap_core)

    pair = 2 * UNIT
    height = last.shape[0]
    window = -(-(height + LANES - 8) // LANES) * LANES
    tile = jnp.minimum(last_row // LANES, (padded - window) // LANES).astype(jnp.int32)

    def forward(rows, name):
        return pl.pallas_call(
            forward_kernel,
            out_shape=(
                shape((half, sections * UNIT, columns), F32),
                shape((half, sections * UNIT, window), BF),
                shape((half, sections, LANES), F32),
            ),
            grid_spec=pltpu.PrefetchScalarGridSpec(
                num_scalar_prefetch=1,
                grid=(half // 2,),
                in_specs=[
                    pl.BlockSpec((sections, pair, padded), lambda i, tile: (0, i, 0)),
                    pl.BlockSpec((padded, columns), lambda i, tile: (0, 0)),
                ],
                out_specs=(
                    pl.BlockSpec((2, sections * UNIT, columns), lambda i, tile: (i, 0, 0)),
                    pl.BlockSpec((2, sections * UNIT, window), lambda i, tile: (i, 0, 0)),
                    pl.BlockSpec((2, sections, LANES), lambda i, tile: (i, 0, 0)),
                ),
            ),
            compiler_params=PARAMS,
            cost_estimate=FREE,
            name=name,
        )(tile.reshape(1), rows, early_weight)

    own_main, own_window, own_notes = forward(from_own, "forward_own")
    other_main, other_window, other_notes = forward(from_other, "forward_other")
    last_window = lax.dynamic_update_slice_in_dim(
        jnp.zeros((window, columns), BF), last, last_row - tile * LANES, 0
    )
    partial = pl.pallas_call(
        tail_kernel,
        out_shape=pltpu.HBM((units, sections * UNIT, columns), BF),
        in_specs=[SMEM] + [VMEM] * 5,
        out_specs=ANY,
        scratch_shapes=[
            pltpu.VMEM((units, sections * UNIT, columns), BF),
            pltpu.SemaphoreType.DMA((units,)),
        ],
        compiler_params=PARAMS,
        cost_estimate=FREE,
        name="tail",
    )(core_index, own_window, other_window, last_window, own_main, other_main)
    partial = lax.all_to_all(partial, along_first, 0, 0, tiled=True)
    weight = lax.dynamic_update_slice_in_dim(early_weight, last, last_row, 0)

    at = LANES - (padded - chunk)
    table = jnp.where(
        core == 0,
        jnp.concatenate([own_notes, other_notes]),
        jnp.concatenate([other_notes, own_notes]),
    )
    table = jnp.swapaxes(table[:, :, at : at + 3], 0, 1).astype(jnp.int32)
    here = lax.dynamic_slice_in_dim(table, section, 1, 1)[:, 0]
    has = here[:, 1] > 0
    spots = jnp.arange(sections)
    where = fill_places(here[:, 2], has, spots)
    has = has.astype(jnp.int32)

    share = units // tensors
    back = jnp.array([0, 0, 1, 1, -1, -1, 2, 2])
    from_section = (section // 2 - back) % along * 2 + (y_lo ^ jnp.array([0, 1] * 4))
    run = jnp.sum(
        jnp.where(from_section[:, None, None] == spots, table[None, :, :, 0], 0), axis=2
    )
    side = run // share
    pick = (side % 2 == core) * along + spots // 2
    pick = ((pick * 2 + side // 2) * 2 + spots % 2) * share + run % share
    pick = pick.reshape(-1).astype(jnp.int32)
    hat, hat_inv = pl.pallas_call(
        hat_kernel,
        out_shape=(shape((share * UNIT, depth), F32), shape((share * UNIT, LANES), F32)),
        grid_spec=pltpu.PrefetchScalarGridSpec(
            num_scalar_prefetch=1,
            grid=(share,),
            in_specs=[ANY, pl.BlockSpec((UNIT, depth), lambda i, first: (first[0] + i, 0))],
            out_specs=(
                pl.BlockSpec((UNIT, depth), lambda i, first: (i, 0)),
                pl.BlockSpec((UNIT, LANES), lambda i, first: (i, 0)),
            ),
        ),
        compiler_params=WIDE,
        cost_estimate=FREE,
        name="vision_hat",
    )((tensor * share).reshape(1).astype(jnp.int32), table, vision_rows)
    upstream, text_stat = pl.pallas_call(
        prepare_kernel,
        out_shape=(pltpu.HBM((slots, columns), F32), shape((8, LANES), F32)),
        in_specs=[VMEM] * 3,
        out_specs=(VMEM, VMEM),
        compiler_params=PARAMS,
        cost_estimate=FREE,
        name="prepare",
    )(text_rows, out_cotangent, after(text_gain_row, hat_inv))
    feature, slope, run_upstream, stat = pl.pallas_call(
        slots_kernel,
        out_shape=(
            shape((slots, columns), BF),
            shape((slots, columns), F32),
            shape((slots, columns), F32),
            shape((8, LANES), F32),
        ),
        in_specs=[SMEM, VMEM, pl.BlockSpec(memory_space=pltpu.HBM), VMEM],
        out_specs=(VMEM,) * 4,
        scratch_shapes=[pltpu.VMEM((slots, columns), F32), pltpu.SemaphoreType.DMA],
        compiler_params=PARAMS,
        cost_estimate=FREE,
        name="slots",
    )(after(where, pick, hat_inv), partial, upstream, text_stat)
    stats = [stat] + [
        lax.ppermute(stat, ("y_hi", "core"), [(i, i ^ turn) for i in range(tensors)])
        for turn in range(1, tensors)
    ]
    grads = pl.pallas_call(
        functools.partial(grad_kernel, width),
        out_shape=shape((sections, UNIT, columns), BF),
        in_specs=[SMEM] + [VMEM] * (3 + tensors),
        out_specs=VMEM,
        compiler_params=PARAMS,
        cost_estimate=FREE,
        name="grads",
    )(has, feature, slope, run_upstream, *stats)
    def turn(block, dx, dy=0):
        moves = [
            (i, (i // along ^ dy) * along + (i + dx) % along) for i in range(sections)
        ]
        return lax.ppermute(block, ("y_lo", "x"), moves)

    across = turn(grads, 0, 1)
    left, right = lax.optimization_barrier((turn(grads, 1), turn(grads, -1)))
    left_across, right_across = turn(across, 1), turn(across, -1)
    opposite, opposite_across = turn(left, 1), turn(right_across, -1)
    blocks = [grads, across, left, left_across, right, right_across, opposite, opposite_across]
    grads = pl.pallas_call(
        arrange_kernel,
        out_shape=shape((sections * sections, UNIT, columns), BF),
        in_specs=[SMEM] + [VMEM] * sections,
        out_specs=VMEM,
        compiler_params=PARAMS,
        cost_estimate=FREE,
        name="arrange",
    )(pick, *blocks)
    normed = pl.pallas_call(
        functools.partial(normed_kernel, width),
        out_shape=shape((slots, columns), BF),
        in_specs=[SMEM, SMEM] + [VMEM] * (3 + tensors),
        out_specs=VMEM,
        compiler_params=PARAMS,
        cost_estimate=FREE,
        name="normed",
    )(where, has, text_rows, feature, text_gain_row, *stats)

    peers = sections * 2
    quarter = sections * units // 4

    def product(first, count, dtype, name):
        return pl.pallas_call(
            back_kernel,
            out_shape=shape((count * quarter * UNIT, padded), dtype),
            grid=(count,),
            in_specs=[
                pl.BlockSpec((quarter, UNIT, columns), lambda i: (first + i, 0, 0)),
                pl.BlockSpec((padded, columns), lambda i: (0, 0)),
            ],
            out_specs=pl.BlockSpec((quarter * UNIT, padded), lambda i: (i, 0)),
            compiler_params=PARAMS,
            cost_estimate=FREE,
            name=name,
        )(grads, weight)

    got = [
        lax.ppermute(product(h, 1, BF, f"give{h}"), "core", swap_core) for h in range(2)
    ]
    total = pl.pallas_call(
        join_kernel,
        out_shape=pltpu.HBM((peers, share * UNIT, padded), BF),
        grid=(2,),
        in_specs=[pl.BlockSpec((quarter * UNIT, padded), lambda i: (i, 0))]
        + [pl.BlockSpec((quarter * UNIT, padded), lambda i: (0, 0))] * 2,
        out_specs=pl.BlockSpec((sections, share * UNIT, padded), lambda i: (i, 0, 0)),
        compiler_params=PARAMS,
        cost_estimate=FREE,
        name="join",
    )(product(2, 2, F32, "keep"), *got)
    back = lax.all_to_all(total, ("x", "y_hi", "y_lo"), 0, 0, tiled=True)
    order = []
    for y_lo in range(2):
        for x in range(along):
            order.append([(x * 2 + y_hi) * 2 + y_lo for y_hi in range(2)])
    vision_grad = pl.pallas_call(
        functools.partial(final_kernel, chunk, order),
        out_shape=shape((share * UNIT, depth), BF),
        grid=(share,),
        in_specs=[
            pl.BlockSpec((peers, UNIT, padded), lambda i: (0, i, 0)),
            pl.BlockSpec((UNIT, depth), lambda i: (i, 0)),
            pl.BlockSpec((UNIT, LANES), lambda i: (i, 0)),
            pl.BlockSpec((depth,), lambda i: (0,)),
        ],
        out_specs=pl.BlockSpec((UNIT, depth), lambda i: (i, 0)),
        compiler_params=PARAMS,
        cost_estimate=FREE,
        name="vision_back",
    )(back, hat, hat_inv, vision_gain)
    return normed, vision_grad


def solution(mesh):
    mesh = Mesh(
        mesh.devices.reshape(2, mesh.shape["section"] // 2, mesh.shape["dp"], -1, 2),
        ("y_lo", "x", "dp", "y_hi", "core"),
    )
    rows, tensor = ("y_lo", "x", "dp"), ("y_hi", "core")
    in_specs = (
        P(rows, None),
        P(),
        P(),
        P(rows, tensor),
        P(rows, tensor),
        P(tensor),
        P(rows),
        P(rows, tensor),
    )
    out_specs = (P(rows, tensor), P((*rows, *tensor), None))

    def program(*args):
        body = functools.partial(shards, args[4].shape[1])
        return jax.shard_map(
            body, mesh=mesh, in_specs=in_specs, out_specs=out_specs, check_vma=False
        )(*args)

    return program
```

```python
import functools

import jax
import jax.numpy as jnp
from jax import lax
from jax.experimental import pallas as pl
from jax.experimental.pallas import tpu as pltpu
from jax.sharding import Mesh
from jax.sharding import PartitionSpec as P

UNIT = 16
LANES = 128
VISION_EPS = 1e-05
EPSILON = 1e-06
HALF_ROOT = 0.7071067811865476
INV_ROOT_TWO_PI = 0.3989422804014327
BF = jnp.bfloat16
F32 = jnp.float32
VMEM = pl.BlockSpec(memory_space=pltpu.VMEM)
SMEM = pl.BlockSpec(memory_space=pltpu.SMEM)
ANY = pl.BlockSpec(memory_space=pl.ANY)
FREE = pl.CostEstimate(flops=0, transcendentals=0, bytes_accessed=0)
PARAMS = pltpu.CompilerParams(vmem_limit_bytes=40 * 2**20)
WIDE = pltpu.CompilerParams(vmem_limit_bytes=60 * 2**20)
NT = (((1,), (1,)), ((), ()))


def shape(dims, dtype):
    return jax.ShapeDtypeStruct(dims, dtype)


def run_order(slot_ref, units, section_slots, along):
    slots = [slot_ref[u * UNIT] for u in range(units)]
    alive = [slot >= 0 for slot in slots]
    target = [jnp.maximum(slot, 0) // section_slots for slot in slots]
    target = [t % along * 2 + t // along for t in target]
    place = [jnp.where(a, t, -1) for a, t in zip(alive, target)]
    taken = []
    for spot in range(units):
        hits = [jnp.where(p == spot, 1, 0) for p in place]
        taken.append(functools.reduce(lambda a, b: a + b, hits))
    dead_rank = jnp.int32(0)
    for u in range(units):
        free_rank = jnp.int32(0)
        filler = jnp.int32(0)
        for spot in range(units):
            free = 1 - taken[spot]
            filler = jnp.where((free > 0) & (free_rank == dead_rank), spot, filler)
            free_rank = free_rank + free
        place[u] = jnp.where(alive[u], place[u], filler)
        dead_rank = dead_rank + jnp.where(alive[u], 0, 1)
    return slots, alive, place


def norm_kernel(
    chunk, own_slots, section_slots, along, slot_ref, core_ref, rows_ref, gain_ref, bias_ref, out_ref, held, made, sems, out_sems
):
    parts, high, padded = out_ref.shape
    half = high // UNIT
    units = 2 * half
    slots, alive, place = run_order(slot_ref, units, section_slots, along)
    notes = []
    for i in range(half):
        run, slot, live = jnp.int32(0), jnp.int32(0), jnp.int32(0)
        for u in range(units):
            here = place[u] == core_ref[0] * half + i
            run = jnp.where(here, u, run)
            slot = jnp.where(here, slots[u], slot)
            live = jnp.where(here & alive[u], 1, live)
        spot = jnp.where(live > 0, slot // UNIT % (own_slots // UNIT), 0)
        notes.append((run, live, spot))
    copies = []
    for i, (run, _, _) in enumerate(notes):
        rows = pl.ds(pl.multiple_of(run * UNIT, UNIT), UNIT)
        copies.append(pltpu.make_async_copy(rows_ref.at[rows], held.at[i], sems.at[i]))
        copies[i].start()
    gain, bias = gain_ref[...].reshape(1, -1), bias_ref[...].reshape(1, -1)
    lane = lax.broadcasted_iota(jnp.int32, (UNIT, padded - chunk), 1)
    for i, (run, live, spot) in enumerate(notes):
        copies[i].wait()
        wide = held[i].astype(F32)
        centered = wide - jnp.mean(wide, axis=1, keepdims=True)
        inv = lax.rsqrt(jnp.mean(centered * centered, axis=1, keepdims=True) + VISION_EPS)
        normed = (centered * inv * gain + bias).astype(BF)
        note = jnp.where(lane == 0, run, jnp.where(lane == 1, live, spot)).astype(F32).astype(BF)
        for k in range(parts):
            at = (k % 2 * (parts // 2) + k // 2) * chunk
            made[i, k] = jnp.concatenate([normed[:, at : at + chunk], note], axis=1)
        target = out_ref.at[:, pl.ds(i * UNIT, UNIT)]
        copies.append(pltpu.make_async_copy(made.at[i], target, out_sems.at[i]))
        copies[-1].start()
    for copy in copies[half:]:
        copy.wait()


def forward_kernel(tile_ref, rows_ref, weight_ref, out_ref, window_ref, note_ref):
    sections, high, depth = rows_ref.shape
    at = pl.ds(pl.multiple_of(tile_ref[0] * LANES, LANES), window_ref.shape[2])
    product = jnp.dot(
        rows_ref[...].reshape(sections * high, depth), weight_ref[...], preferred_element_type=F32
    )
    product = product.reshape(sections, high, product.shape[1])
    for j in range(high // UNIT):
        run = slice(j * UNIT, (j + 1) * UNIT)
        out_ref[j] = product[:, run].reshape(sections * UNIT, -1)
        window_ref[j] = rows_ref[:, run, at].reshape(sections * UNIT, -1)
        heads = [rows_ref[s, run, depth - LANES :][:1] for s in range(sections)]
        note_ref[j] = jnp.concatenate([head.astype(F32) for head in heads], axis=0)


def tail_kernel(
    core_ref, own_window_ref, other_window_ref, weight_ref, own_ref, other_ref, out_ref, made, sems
):
    half = own_ref.shape[0]
    halves = ((core_ref[0], own_window_ref, own_ref), (1 - core_ref[0], other_window_ref, other_ref))
    copies = []
    for side, window_ref, main_ref in halves:
        for j in range(half):
            n = len(copies)
            product = jnp.dot(window_ref[j], weight_ref[...], preferred_element_type=F32)
            made[n] = (main_ref[j] + product).astype(BF)
            target = out_ref.at[side * half + j]
            copies.append(pltpu.make_async_copy(made.at[n], target, sems.at[n]))
            copies[n].start()
    for copy in copies:
        copy.wait()


def prepare_kernel(text_ref, cot_ref, gain_ref, upstream_ref, stat_ref):
    upstream_ref[...] = cot_ref[...].astype(F32) * gain_ref[...]
    text = text_ref[...].astype(F32)
    square = jnp.sum(text * text, axis=1, keepdims=True)
    square = jnp.broadcast_to(square, (square.shape[0], LANES))
    stat_ref[...] = jnp.transpose(square)[: stat_ref.shape[0]]


def slots_kernel(
    place_ref, parts_ref, upstream_ref, text_stat_ref, feature_ref, slope_ref, grad_ref, stat_ref, held, sem
):
    copy = pltpu.make_async_copy(upstream_ref, held, sem)
    copy.start()
    runs = feature_ref.shape[0] // UNIT
    for s in range(runs):
        rows = slice(s * UNIT, (s + 1) * UNIT)
        projected = parts_ref[0, rows].astype(F32)
        for k in range(1, parts_ref.shape[0]):
            projected = projected + parts_ref[k, rows].astype(F32)
        gate = 0.5 * (1.0 + lax.erf(projected * HALF_ROOT))
        feature_ref[rows] = (projected * gate).astype(BF)
        slope_ref[rows] = gate + projected * jnp.exp(-0.5 * projected * projected) * INV_ROOT_TWO_PI
    copy.wait()
    lane = lax.broadcasted_iota(jnp.int32, (UNIT, LANES), 1)
    stats = []
    for s in range(runs):
        rows = slice(s * UNIT, (s + 1) * UNIT)
        at = pl.ds(pl.multiple_of(place_ref[s] * UNIT, UNIT), UNIT)
        wide, upstream = feature_ref[rows].astype(F32), held[at]
        grad_ref[rows] = upstream
        square = jnp.sum(wide * wide, axis=1, keepdims=True)
        cross = jnp.sum(upstream * wide, axis=1, keepdims=True)
        stats.append(jnp.where(lane == 0, square, cross))
    stat = jnp.transpose(jnp.concatenate(stats, axis=0))[: stat_ref.shape[0]]
    row = lax.broadcasted_iota(jnp.int32, stat.shape, 0)
    stat_ref[...] = jnp.where(row == 2, text_stat_ref[...], stat)


def row_scales(stat_refs, width):
    stat = sum(ref[...] for ref in stat_refs) / width
    pad = jnp.zeros((LANES - stat.shape[0], LANES), F32)
    return jnp.transpose(jnp.concatenate([stat, pad], axis=0))


def grad_kernel(
    width, live_ref, feature_ref, slope_ref, upstream_ref, *refs
):
    stat_refs, grad_ref = refs[:-1], refs[-1]
    stat = row_scales(stat_refs, width)
    for s in range(feature_ref.shape[0] // UNIT):
        rows = slice(s * UNIT, (s + 1) * UNIT)
        inv, cross = lax.rsqrt(stat[rows, 0:1] + EPSILON), stat[rows, 1:2]
        wide = feature_ref[rows].astype(F32)
        hidden_grad = (inv * (upstream_ref[rows] - wide * inv * inv * cross)).astype(BF)
        grad = (hidden_grad.astype(F32) * slope_ref[rows]).astype(BF)
        grad = jnp.where(live_ref[s] > 0, grad, jnp.zeros_like(grad))
        grad_ref[s] = grad


def normed_kernel(
    width, place_ref, live_ref, text_ref, feature_ref, gain_ref, *refs
):
    stat_refs, normed_ref = refs[:-1], refs[-1]
    stat = row_scales(stat_refs, width)
    inv = lax.rsqrt(stat[:, 2:3] + EPSILON)
    normed_ref[...] = (text_ref[...].astype(F32) * inv * gain_ref[...]).astype(BF)
    for s in range(feature_ref.shape[0] // UNIT):
        rows = slice(s * UNIT, (s + 1) * UNIT)
        at = pl.ds(pl.multiple_of(place_ref[s] * UNIT, UNIT), UNIT)

        @pl.when(live_ref[s] > 0)
        def _(rows=rows, at=at):
            inv = lax.rsqrt(stat[rows, 0:1] + EPSILON)
            normed_ref[at] = (feature_ref[rows].astype(F32) * inv * gain_ref[...]).astype(BF)


def arrange_kernel(pick_ref, *refs):
    blocks, out_ref = refs[:-1], refs[-1]
    for b, ref in enumerate(blocks):
        for s in range(ref.shape[0]):
            out_ref[pick_ref[b * ref.shape[0] + s]] = ref[s]


def back_kernel(grads_ref, weight_ref, out_ref):
    grad = grads_ref[...].reshape(out_ref.shape[0], -1)
    product = lax.dot_general(grad, weight_ref[...], NT, preferred_element_type=F32)
    out_ref[...] = product.astype(out_ref.dtype)


def join_kernel(own_ref, low_ref, high_ref, out_ref):
    got = jnp.where(pl.program_id(0) == 0, low_ref[...], high_ref[...])
    total = (own_ref[...] + got.astype(F32)).astype(BF)
    targets, share, _ = out_ref.shape
    for j in range(targets):
        out_ref[j] = total[j * share : (j + 1) * share]


def hat_kernel(first_ref, table_ref, rows_ref, hat_ref, inv_ref):
    del table_ref
    wide = rows_ref[...].astype(F32)
    centered = wide - jnp.mean(wide, axis=1, keepdims=True)
    inv = lax.rsqrt(jnp.mean(centered * centered, axis=1, keepdims=True) + VISION_EPS)
    hat_ref[...] = centered * inv
    inv_ref[...] = jnp.broadcast_to(inv, inv_ref.shape)


def final_kernel(chunk, order, parts_ref, hat_ref, inv_ref, gain_ref, out_ref):
    grad = jnp.concatenate(
        [
            parts_ref[a][:, :chunk].astype(F32) + parts_ref[b][:, :chunk].astype(F32)
            for a, b in order
        ],
        axis=1,
    )
    hat, inv = hat_ref[...], inv_ref[:, 0:1]
    weighted = grad * gain_ref[...].reshape(1, -1)
    weighted_mean = jnp.mean(weighted, axis=1, keepdims=True)
    cross = jnp.mean(weighted * hat, axis=1, keepdims=True)
    out_ref[...] = (inv * (weighted - weighted_mean - hat * cross)).astype(BF)


def ring_gather(block, rows, beside):
    groups = lax.axis_size("dp")
    me = lax.axis_index("dp")
    height = block.shape[0]
    turn = 1 - 2 * lax.axis_index("core")
    ring = ("dp", "core")
    up = [
        (i * 2 + core, (i + 1 - 2 * core) % groups * 2 + core)
        for i in range(groups)
        for core in range(2)
    ]
    down = [(target, source) for source, target in up]
    out = jnp.zeros((rows, block.shape[1]), block.dtype)

    def put(out, piece, owner):
        return lax.dynamic_update_slice_in_dim(out, piece, owner % groups * height, 0)

    out = put(out, block, me)
    rising = falling = block
    for hop in range(1, (groups - 1) // 2 + 1):
        rising = lax.ppermute(rising, ring, up)
        falling = lax.ppermute(falling, ring, down)
        out, rising, falling = lax.optimization_barrier((out, rising, falling))
        if hop == 1:
            rising, falling, beside = lax.optimization_barrier((rising, falling, beside))
        out = put(out, rising, me - hop * turn + groups)
        out = put(out, falling, me + hop * turn + groups)
    last = lax.ppermute(rising, ring, up)
    owner = (me + groups // 2) % groups
    return out, last, owner * height, rising, falling, beside


def after(value, *marks):
    return lax.optimization_barrier((value, marks))[0]


def fill_places(wanted, alive, places):
    taken = jnp.any((wanted[..., :, None] == places) & alive[..., :, None], axis=-2)
    free_rank = jnp.cumsum(~taken, axis=-1) - 1
    dead_rank = jnp.cumsum(~alive, axis=-1) - 1
    fits = (~taken)[..., None, :] & (free_rank[..., None, :] == dead_rank[..., :, None])
    filler = jnp.sum(jnp.where(fits, places, 0), axis=-1)
    return jnp.where(alive, wanted, filler).astype(jnp.int32)


def inverse(place, places):
    return jnp.sum(
        jnp.where(place[..., :, None] == places, places[:, None], 0), axis=-2
    ).astype(jnp.int32)


def shards(
    width, vision_rows, vision_gain, vision_bias, proj_weight, text_rows, text_gain, slot_of_row, out_cotangent
):
    along = lax.axis_size("x")
    sections = 2 * along
    along_first = ("x", "y_lo")
    groups = lax.axis_size("dp")
    tensors = 2 * lax.axis_size("y_hi")
    rows, depth = vision_rows.shape
    slots, columns = text_rows.shape
    units = rows // UNIT
    chunk = depth // sections
    padded = -(-(chunk + 3) // LANES) * LANES
    y_lo = lax.axis_index("y_lo")
    section = lax.axis_index("x") * 2 + y_lo
    core = lax.axis_index("core")
    tensor = lax.axis_index("y_hi") * 2 + core
    places = jnp.arange(units)
    swap_core = [(0, 1), (1, 0)]

    text_gain_row = text_gain.reshape(1, columns)

    half = units // 2
    core_index = core.reshape(1).astype(jnp.int32)
    sent = pl.pallas_call(
        functools.partial(norm_kernel, chunk, slots, slots * groups, along),
        out_shape=pltpu.HBM((sections, half * UNIT, padded), BF),
        in_specs=[SMEM, SMEM, ANY, VMEM, VMEM],
        out_specs=ANY,
        scratch_shapes=[
            pltpu.VMEM((half, UNIT, depth), BF),
            pltpu.VMEM((half, sections, UNIT, padded), BF),
            pltpu.SemaphoreType.DMA((half,)),
            pltpu.SemaphoreType.DMA((half,)),
        ],
        compiler_params=WIDE,
        cost_estimate=FREE,
        name="vision_norm",
    )(slot_of_row, core_index, vision_rows, vision_gain, vision_bias)
    early_weight, last, last_row, rising, falling, sent = ring_gather(proj_weight, padded, sent)
    from_own = lax.all_to_all(sent, along_first, 0, 0, tiled=True)
    from_own, *_ = lax.optimization_barrier((from_own, rising, falling))
    from_other = lax.ppermute(from_own, "core", swap_core)

    pair = 2 * UNIT
    height = last.shape[0]
    window = -(-(height + LANES - 8) // LANES) * LANES
    tile = jnp.minimum(last_row // LANES, (padded - window) // LANES).astype(jnp.int32)

    def forward(rows, name):
        return pl.pallas_call(
            forward_kernel,
            out_shape=(
                shape((half, sections * UNIT, columns), F32),
                shape((half, sections * UNIT, window), BF),
                shape((half, sections, LANES), F32),
            ),
            grid_spec=pltpu.PrefetchScalarGridSpec(
                num_scalar_prefetch=1,
                grid=(half // 2,),
                in_specs=[
                    pl.BlockSpec((sections, pair, padded), lambda i, tile: (0, i, 0)),
                    pl.BlockSpec((padded, columns), lambda i, tile: (0, 0)),
                ],
                out_specs=(
                    pl.BlockSpec((2, sections * UNIT, columns), lambda i, tile: (i, 0, 0)),
                    pl.BlockSpec((2, sections * UNIT, window), lambda i, tile: (i, 0, 0)),
                    pl.BlockSpec((2, sections, LANES), lambda i, tile: (i, 0, 0)),
                ),
            ),
            compiler_params=PARAMS,
            cost_estimate=FREE,
            name=name,
        )(tile.reshape(1), rows, early_weight)

    own_main, own_window, own_notes = forward(from_own, "forward_own")
    other_main, other_window, other_notes = forward(from_other, "forward_other")
    last_window = lax.dynamic_update_slice_in_dim(
        jnp.zeros((window, columns), BF), last, last_row - tile * LANES, 0
    )
    partial = pl.pallas_call(
        tail_kernel,
        out_shape=pltpu.HBM((units, sections * UNIT, columns), BF),
        in_specs=[SMEM] + [VMEM] * 5,
        out_specs=ANY,
        scratch_shapes=[
            pltpu.VMEM((units, sections * UNIT, columns), BF),
            pltpu.SemaphoreType.DMA((units,)),
        ],
        compiler_params=PARAMS,
        cost_estimate=FREE,
        name="tail",
    )(core_index, own_window, other_window, last_window, own_main, other_main)
    partial = lax.all_to_all(partial, along_first, 0, 0, tiled=True)
    weight = lax.dynamic_update_slice_in_dim(early_weight, last, last_row, 0)

    at = LANES - (padded - chunk)
    table = jnp.where(
        core == 0,
        jnp.concatenate([own_notes, other_notes]),
        jnp.concatenate([other_notes, own_notes]),
    )
    table = jnp.swapaxes(table[:, :, at : at + 3], 0, 1).astype(jnp.int32)
    here = lax.dynamic_slice_in_dim(table, section, 1, 1)[:, 0]
    has = here[:, 1] > 0
    spots = jnp.arange(sections)
    where = fill_places(here[:, 2], has, spots)
    has = has.astype(jnp.int32)

    share = units // tensors
    back = jnp.array([0, 0, 1, 1, -1, -1, 2, 2])
    from_section = (section // 2 - back) % along * 2 + (y_lo ^ jnp.array([0, 1] * 4))
    run = jnp.sum(
        jnp.where(from_section[:, None, None] == spots, table[None, :, :, 0], 0), axis=2
    )
    side = run // share
    pick = (side % 2 == core) * along + spots // 2
    pick = ((pick * 2 + side // 2) * 2 + spots % 2) * share + run % share
    pick = pick.reshape(-1).astype(jnp.int32)
    hat, hat_inv = pl.pallas_call(
        hat_kernel,
        out_shape=(shape((share * UNIT, depth), F32), shape((share * UNIT, LANES), F32)),
        grid_spec=pltpu.PrefetchScalarGridSpec(
            num_scalar_prefetch=1,
            grid=(share,),
            in_specs=[ANY, pl.BlockSpec((UNIT, depth), lambda i, first: (first[0] + i, 0))],
            out_specs=(
                pl.BlockSpec((UNIT, depth), lambda i, first: (i, 0)),
                pl.BlockSpec((UNIT, LANES), lambda i, first: (i, 0)),
            ),
        ),
        compiler_params=WIDE,
        cost_estimate=FREE,
        name="vision_hat",
    )((tensor * share).reshape(1).astype(jnp.int32), table, vision_rows)
    upstream, text_stat = pl.pallas_call(
        prepare_kernel,
        out_shape=(pltpu.HBM((slots, columns), F32), shape((8, LANES), F32)),
        in_specs=[VMEM] * 3,
        out_specs=(VMEM, VMEM),
        compiler_params=PARAMS,
        cost_estimate=FREE,
        name="prepare",
    )(text_rows, out_cotangent, after(text_gain_row, hat_inv))
    feature, slope, run_upstream, stat = pl.pallas_call(
        slots_kernel,
        out_shape=(
            shape((slots, columns), BF),
            shape((slots, columns), F32),
            shape((slots, columns), F32),
            shape((8, LANES), F32),
        ),
        in_specs=[SMEM, VMEM, pl.BlockSpec(memory_space=pltpu.HBM), VMEM],
        out_specs=(VMEM,) * 4,
        scratch_shapes=[pltpu.VMEM((slots, columns), F32), pltpu.SemaphoreType.DMA],
        compiler_params=PARAMS,
        cost_estimate=FREE,
        name="slots",
    )(after(where, pick, hat_inv), partial, upstream, text_stat)
    stats = [stat] + [
        lax.ppermute(stat, ("y_hi", "core"), [(i, i ^ turn) for i in range(tensors)])
        for turn in range(1, tensors)
    ]
    grads = pl.pallas_call(
        functools.partial(grad_kernel, width),
        out_shape=shape((sections, UNIT, columns), BF),
        in_specs=[SMEM] + [VMEM] * (3 + tensors),
        out_specs=VMEM,
        compiler_params=PARAMS,
        cost_estimate=FREE,
        name="grads",
    )(has, feature, slope, run_upstream, *stats)
    def turn(block, dx, dy=0):
        moves = [
            (i, (i // along ^ dy) * along + (i + dx) % along) for i in range(sections)
        ]
        return lax.ppermute(block, ("y_lo", "x"), moves)

    across = turn(grads, 0, 1)
    left, right = turn(grads, 1), turn(grads, -1)
    across, right = lax.optimization_barrier((across, right))
    left_across, right_across = turn(across, 1), turn(across, -1)
    opposite, opposite_across = turn(left, 1), turn(right_across, -1)
    blocks = [grads, across, left, left_across, right, right_across, opposite, opposite_across]
    grads = pl.pallas_call(
        arrange_kernel,
        out_shape=shape((sections * sections, UNIT, columns), BF),
        in_specs=[SMEM] + [VMEM] * sections,
        out_specs=VMEM,
        compiler_params=PARAMS,
        cost_estimate=FREE,
        name="arrange",
    )(pick, *blocks)
    normed = pl.pallas_call(
        functools.partial(normed_kernel, width),
        out_shape=shape((slots, columns), BF),
        in_specs=[SMEM, SMEM] + [VMEM] * (3 + tensors),
        out_specs=VMEM,
        compiler_params=PARAMS,
        cost_estimate=FREE,
        name="normed",
    )(where, has, text_rows, feature, text_gain_row, *stats)

    peers = sections * 2
    quarter = sections * units // 4

    def product(first, count, dtype, name):
        return pl.pallas_call(
            back_kernel,
            out_shape=shape((count * quarter * UNIT, padded), dtype),
            grid=(count,),
            in_specs=[
                pl.BlockSpec((quarter, UNIT, columns), lambda i: (first + i, 0, 0)),
                pl.BlockSpec((padded, columns), lambda i: (0, 0)),
            ],
            out_specs=pl.BlockSpec((quarter * UNIT, padded), lambda i: (i, 0)),
            compiler_params=PARAMS,
            cost_estimate=FREE,
            name=name,
        )(grads, weight)

    got = [
        lax.ppermute(product(h, 1, BF, f"give{h}"), "core", swap_core) for h in range(2)
    ]
    total = pl.pallas_call(
        join_kernel,
        out_shape=pltpu.HBM((peers, share * UNIT, padded), BF),
        grid=(2,),
        in_specs=[pl.BlockSpec((quarter * UNIT, padded), lambda i: (i, 0))]
        + [pl.BlockSpec((quarter * UNIT, padded), lambda i: (0, 0))] * 2,
        out_specs=pl.BlockSpec((sections, share * UNIT, padded), lambda i: (i, 0, 0)),
        compiler_params=PARAMS,
        cost_estimate=FREE,
        name="join",
    )(product(2, 2, F32, "keep"), *got)
    back = lax.all_to_all(total, ("x", "y_hi", "y_lo"), 0, 0, tiled=True)
    order = []
    for y_lo in range(2):
        for x in range(along):
            order.append([(x * 2 + y_hi) * 2 + y_lo for y_hi in range(2)])
    vision_grad = pl.pallas_call(
        functools.partial(final_kernel, chunk, order),
        out_shape=shape((share * UNIT, depth), BF),
        grid=(share,),
        in_specs=[
            pl.BlockSpec((peers, UNIT, padded), lambda i: (0, i, 0)),
            pl.BlockSpec((UNIT, depth), lambda i: (i, 0)),
            pl.BlockSpec((UNIT, LANES), lambda i: (i, 0)),
            pl.BlockSpec((depth,), lambda i: (0,)),
        ],
        out_specs=pl.BlockSpec((UNIT, depth), lambda i: (i, 0)),
        compiler_params=PARAMS,
        cost_estimate=FREE,
        name="vision_back",
    )(back, hat, hat_inv, vision_gain)
    return normed, vision_grad


def solution(mesh):
    mesh = Mesh(
        mesh.devices.reshape(2, mesh.shape["section"] // 2, mesh.shape["dp"], -1, 2),
        ("y_lo", "x", "dp", "y_hi", "core"),
    )
    rows, tensor = ("y_lo", "x", "dp"), ("y_hi", "core")
    in_specs = (
        P(rows, None),
        P(),
        P(),
        P(rows, tensor),
        P(rows, tensor),
        P(tensor),
        P(rows),
        P(rows, tensor),
    )
    out_specs = (P(rows, tensor), P((*rows, *tensor), None))

    def program(*args):
        body = functools.partial(shards, args[4].shape[1])
        return jax.shard_map(
            body, mesh=mesh, in_specs=in_specs, out_specs=out_specs, check_vma=False
        )(*args)

    return program
```
